32 devices in a mesh: patch: 8 (over z, y), visit: 4 (over x, core).
Axes of the slice: x: 2, y: 2, z: 4, core: 2. Of those that a mesh axis runs over, the one named last changes fastest.
Arguments:
- science: float32 [4096, 2, 128], P(('patch', 'visit')), may hold values from -40 to 40
- inverse_sigma: float32 [4096, 2, 128], P(('patch', 'visit')), may hold values from 0.24 to 3.6
- template: float32 [8, 256, 1024], P('patch', 'visit'), may hold values from -6 to 6
- destination: int32 [4096], P(('patch', 'visit')), may hold values from 0 to 7, as said below
- offsets: int32 [4096, 2], P(('patch', 'visit')), may hold values from 0 to 876, as said below
- visit_local: int32 [4096], P(('patch', 'visit')), may hold values from 0 to 15, as said below
Outputs:
- difference: float32 [4096, 2, 128], P(('patch', 'visit'))
- coefficients: float32 [64, 28], P('visit')
The draws below stay inside these ranges and needn't reach their ends.
Inputs may be any that keep to these rules, and one draw needn't show every extreme that they name: `destination`: in each aligned block of 128 rows no patch is named more than 32 times, and in every draw some patch is named exactly 32 times in every block. `offsets`: column 0 is at most 234, column 1 at most 876. `visit_local`: each aligned block of 128 rows holds every value exactly 128 // 16 times.
All inputs are finite; a program needn't handle non-finite values.
Results may differ from the reference program's by a relative error of at most 0.0098.
Values may be sent and summed in bfloat16 or wider, within the bound.
A program may use at most 64 MiB of HBM per device.

```python
import math
import jax
import jax.numpy as jnp
import numpy as np
from jax import lax

KR = 10
NF = 11
NB = 28
TR = 2
TC = 128
PR = 256
PC = 1024
VIS_DEV = 16
TILES_DEV = 128
HOLDER_TILE_MAX = 32
VISITS = 64
TILES = 4096
N_PATCH = 8
N_VISIT = 4


def holder_arrangement(key):
    holders = N_PATCH * N_VISIT
    slot_grand_count = N_PATCH * HOLDER_TILE_MAX
    hot_total = max(1, N_PATCH // 8)
    ranking = jax.random.permutation(jax.random.fold_in(key, 101), N_PATCH)
    busy_indicator = jnp.where(ranking < hot_total, 1, 0).astype(jnp.int32)
    slot_ids = jnp.arange(slot_grand_count, dtype=jnp.int32)
    extra_credit = jnp.repeat(busy_indicator, HOLDER_TILE_MAX, total_repeat_length=slot_grand_count) * 65536

    def one_holder(holder_key):
        rating_sort_key, shuffle_key, visit_key, row_key, column_key = jax.random.split(holder_key, 5)
        priority_rating = jax.random.randint(rating_sort_key, (slot_grand_count,), 0, 65536, dtype=jnp.int32) + extra_credit
        keyed = priority_rating * slot_grand_count + slot_ids
        chosen = jnp.argsort(-keyed)[:TILES_DEV].astype(jnp.int32)
        placed = jax.random.permutation(shuffle_key, chosen)
        visits = jax.random.permutation(visit_key, jnp.arange(TILES_DEV, dtype=jnp.int32) % VIS_DEV)
        row_starts = jax.random.randint(row_key, (TILES_DEV,), 0, PR - TR - 2 * KR + 1, dtype=jnp.int32)
        column_starts = jax.random.randint(column_key, (TILES_DEV,), 0, PC - TC - 2 * KR + 1, dtype=jnp.int32)
        return (placed // HOLDER_TILE_MAX, visits, jnp.stack([row_starts, column_starts], axis=1))
    holder_keys = jax.random.split(jax.random.fold_in(key, 202), holders)
    patch_ids, visits, starts = jax.vmap(one_holder)(holder_keys)
    return (patch_ids.reshape(TILES), visits.reshape(TILES), starts.reshape(TILES, 2))


def template_field(key):
    base_key = jax.random.fold_in(key, 303)
    first_key = jax.random.fold_in(base_key, 0)
    return jnp.clip(jax.random.normal(first_key, (N_PATCH, PR, PC)), -6.0, 6.0)


def sigma_field(key):
    level_key, pixel_key = jax.random.split(jax.random.fold_in(key, 505))
    level_scale = jnp.exp(jax.random.uniform(level_key, (TILES, 1, 1), minval=math.log(0.3), maxval=math.log(3.0)))
    return level_scale * jax.random.uniform(pixel_key, (TILES, TR, TC), minval=0.8, maxval=1.2)


def draw_destination(key, part):
    patch_ids, visits, starts = holder_arrangement(key)
    return patch_ids


def draw_visit_local(key, part):
    patch_ids, visits, starts = holder_arrangement(key)
    return visits


def draw_offsets(key, part):
    patch_ids, visits, starts = holder_arrangement(key)
    return starts


def draw_template(key, part):
    return template_field(key).astype(jnp.float32)


def draw_inverse_sigma(key, part):
    return sigma_field(key).astype(jnp.float32)


def draw_science(key, part):
    patch_ids, visits, starts = holder_arrangement(key)
    field = template_field(key)
    inverse = sigma_field(key)
    tile_ids = jnp.arange(TILES, dtype=jnp.int32)
    global_visit = tile_ids // TILES_DEV % N_VISIT * VIS_DEV + visits
    kernel_key, noise_key = jax.random.split(jax.random.fold_in(key, 404))
    center = jnp.zeros((3, 3), jnp.float32).at[1, 1].set(1.0)
    kernels = 0.25 * jax.random.normal(kernel_key, (VISITS, 3, 3)) + center[None]
    reach = KR - 1
    span_count = 2 * reach + 1
    width_key, strength_key = jax.random.split(jax.random.fold_in(key, 606))
    broad_widths = KR * jax.random.uniform(width_key, (VISITS, 1), minval=0.25, maxval=0.4)
    broad_strengths = jax.random.uniform(strength_key, (VISITS, 1), minval=0.8, maxval=1.2)
    tap_points = jnp.arange(-reach, reach + 1, dtype=jnp.float32)[None, :]
    bells = jnp.exp(-tap_points * tap_points / (2.0 * broad_widths * broad_widths))
    bells = bells * jnp.sqrt(broad_strengths / jnp.sum(bells * bells, axis=1, keepdims=True))
    amplitude = 1.0 + 2.0 * patch_ids.astype(jnp.float32) / max(N_PATCH - 1, 1)

    def one_tile(patch_id, start_pair, weights_three, bell_taps, scale_value):
        patch_field = lax.dynamic_index_in_dim(field, patch_id, 0, keepdims=False)
        window = lax.dynamic_slice(patch_field, (start_pair[0] + KR - 1, start_pair[1] + KR - 1), (TR + 2, TC + 2))
        running_sum = jnp.zeros((TR, TC), jnp.float32)
        for row_shift in range(3):
            for col_shift in range(3):
                running_sum = running_sum + weights_three[row_shift, col_shift] * window[row_shift:row_shift + TR, col_shift:col_shift + TC]
        wide_window = lax.dynamic_slice(patch_field, (start_pair[0] + KR - reach, start_pair[1] + KR - reach), (TR + 2 * reach, TC + 2 * reach))
        row_pass = jnp.zeros((TR, TC + 2 * reach), jnp.float32)
        for row_shift in range(span_count):
            row_pass = row_pass + bell_taps[row_shift] * wide_window[row_shift:row_shift + TR, :]
        broad_part = jnp.zeros((TR, TC), jnp.float32)
        for col_shift in range(span_count):
            broad_part = broad_part + bell_taps[col_shift] * row_pass[:, col_shift:col_shift + TC]
        return scale_value * (running_sum + broad_part)
    block_size = TILES_DEV * N_VISIT
    block_count = TILES // block_size

    def shaped(values):
        return values.reshape((block_count, block_size) + values.shape[1:])
    truth = lax.map(lambda pieces: jax.vmap(one_tile)(pieces[0], pieces[1], pieces[2], pieces[3], pieces[4]), (shaped(patch_ids), shaped(starts), shaped(kernels[global_visit]), shaped(bells[global_visit]), shaped(amplitude)))
    truth = truth.reshape(TILES, TR, TC)
    noise = jax.random.normal(noise_key, (TILES, TR, TC))
    return jnp.clip(truth + 0.3 * noise / inverse, -40.0, 40.0).astype(jnp.float32)


def setup_inputs(seed: int = 0) -> dict:
    keys = jax.random.split(jax.random.key(seed), 7)
    science = draw_science(jax.random.fold_in(keys[6], 71), 0)
    inverse_sigma = draw_inverse_sigma(jax.random.fold_in(keys[6], 71), 0)
    template = draw_template(jax.random.fold_in(keys[6], 71), 0)
    destination = draw_destination(jax.random.fold_in(keys[6], 71), 0)
    offsets = draw_offsets(jax.random.fold_in(keys[6], 71), 0)
    visit_local = draw_visit_local(jax.random.fold_in(keys[6], 71), 0)
    return {"science": science, "inverse_sigma": inverse_sigma, "template": template, "destination": destination, "offsets": offsets, "visit_local": visit_local}


gauss_widths = (1.0, 2.0, 4.0)
poly_degrees = (4, 2, 2)

def filter_table(radius):
    tap_points = np.arange(-radius, radius + 1) * 1.0
    raw_columns = []
    for width_value, degree in zip(gauss_widths, poly_degrees):
        bell_curve = np.exp(-tap_points * tap_points / (2.0 * width_value * width_value))
        for power_index in range(degree + 1):
            raw_columns.append(bell_curve * (tap_points / radius) ** power_index)
    orthonormal = []
    for column in raw_columns:
        vector = column.copy()
        for repeat_index in range(2):
            for earlier in orthonormal:
                vector = vector - np.dot(earlier, vector) * earlier
        orthonormal.append(vector / np.sqrt(np.dot(vector, vector)))
    return np.stack(orthonormal, axis=1).astype(np.float32)

def pair_layout():
    column_ids = []
    row_ids = []
    filter_runs = []
    offset = 0
    for degree in poly_degrees:
        for first_index in range(degree + 1):
            filter_runs.append((offset + first_index, offset, offset + degree - first_index + 1))
            for second_index in range(degree + 1 - first_index):
                column_ids.append(offset + first_index)
                row_ids.append(offset + second_index)
        offset += degree + 1
    return (column_ids, row_ids, filter_runs)

def rounded(values):
    return lax.optimization_barrier(values.astype(jnp.bfloat16)).astype(jnp.float32)

def reference(science, inverse_sigma, template, destination, offsets, visit_local):
    column_ids, row_ids, filter_runs = pair_layout()
    taps_count = 2 * KR + 1
    filter_values = rounded(jnp.asarray(filter_table(KR)).astype(jnp.float32))
    column_index = jnp.asarray(column_ids, dtype=jnp.int32)
    row_index = jnp.asarray(row_ids, dtype=jnp.int32)
    template_round = rounded(template)
    weights = rounded(inverse_sigma)
    scaled_science = rounded(science * inverse_sigma)
    tile_ids = jnp.arange(TILES, dtype=jnp.int32)
    visit_of = tile_ids // TILES_DEV % N_VISIT * VIS_DEV + visit_local
    height = TR + 2 * KR
    breadth = TC + 2 * KR
    block_size = TILES_DEV * N_VISIT
    block_count = TILES // block_size
    highest = lax.Precision.HIGHEST

    def cut_window(patch_id, row_at, column_at):
        starts = (patch_id.astype(jnp.int32), row_at.astype(jnp.int32), column_at.astype(jnp.int32))
        return lax.dynamic_slice(template_round, starts, (1, height, breadth))[0]

    def filtered_of(windows):
        running_sum = windows[:, None, 0:TR, :] * filter_values[0][None, :, None, None]
        for shift_index in range(1, taps_count):
            running_sum = running_sum + windows[:, None, shift_index:shift_index + TR, :] * filter_values[shift_index][None, :, None, None]
        return rounded(running_sum)

    def images_of(filtered):
        chosen = filtered[:, row_index]
        column_weights = filter_values[:, column_index]
        running_sum = chosen[..., 0:TC] * column_weights[0][None, :, None, None]
        for shift_index in range(1, taps_count):
            running_sum = running_sum + chosen[..., shift_index:shift_index + TC] * column_weights[shift_index][None, :, None, None]
        return running_sum

    def shaped(values):
        return values.reshape((block_count, block_size) + values.shape[1:])

    def windows_of(patch_ids, offset_rows):
        return jax.vmap(cut_window)(patch_ids, offset_rows[:, 0], offset_rows[:, 1])

    def first_pass(carry, pieces):
        gram_sum, right_sum = carry
        patch_ids, offset_rows, block_visits, block_weights, block_scaled = pieces
        images = images_of(filtered_of(windows_of(patch_ids, offset_rows)))
        design = rounded(images * block_weights[:, None])
        design = jnp.concatenate([design, block_weights[:, None]], axis=1).reshape(block_size, NB, TR * TC)
        gram_matrix = jnp.einsum('nkp,nlp->nkl', design, design, precision=highest)
        right_vector = jnp.einsum('nkp,np->nk', design, block_scaled.reshape(block_size, TR * TC), precision=highest)
        gram_sum = gram_sum + jax.ops.segment_sum(gram_matrix, block_visits, num_segments=VISITS)
        right_sum = right_sum + jax.ops.segment_sum(right_vector, block_visits, num_segments=VISITS)
        return ((gram_sum, right_sum), None)
    start = (jnp.zeros((VISITS, NB, NB), jnp.float32), jnp.zeros((VISITS, NB), jnp.float32))
    (gram_total, right_total), unused = lax.scan(first_pass, start, (shaped(destination), shaped(offsets), shaped(visit_of), shaped(weights), shaped(scaled_science)))
    coefficients = jnp.linalg.solve(gram_total, right_total[..., None])[..., 0]
    mixing = jnp.zeros((VISITS, NF, NF), jnp.float32).at[:, column_index, row_index].set(coefficients[:, :NB - 1])

    def second_pass(pieces):
        patch_ids, offset_rows, block_visits, block_science = pieces
        filtered = filtered_of(windows_of(patch_ids, offset_rows))
        combined = jnp.einsum('nab,nbix->naix', mixing[block_visits], filtered, precision=highest)
        running_sum = jnp.einsum('a,naij->nij', filter_values[0], combined[..., 0:TC], precision=highest)
        for shift_index in range(1, taps_count):
            running_sum = running_sum + jnp.einsum('a,naij->nij', filter_values[shift_index], combined[..., shift_index:shift_index + TC], precision=highest)
        model = rounded(running_sum + coefficients[block_visits, NB - 1][:, None, None])
        return block_science - model
    difference = lax.map(second_pass, (shaped(destination), shaped(offsets), shaped(visit_of), shaped(science)))
    return (difference.reshape(TILES, TR, TC), coefficients)
```

```python
import functools

import jax
import jax.numpy as jnp
import numpy as np
from jax import lax
from jax.experimental import pallas as pl
from jax.experimental.pallas import tpu as pltpu
from jax.sharding import PartitionSpec as P

KR = 10
NF = 11
NB = 28
VIS_DEV = 16
ROWS = 32
RHS = NB
GROUP = 8
LANES = 128
VMEM_BYTES = 60 * 1024 * 1024


gauss_widths = (1.0, 2.0, 4.0)
poly_degrees = (4, 2, 2)


def filter_table(radius):
    tap_points = np.arange(-radius, radius + 1) * 1.0
    raw_columns = []
    for width_value, degree in zip(gauss_widths, poly_degrees):
        bell_curve = np.exp(-tap_points * tap_points / (2.0 * width_value * width_value))
        for power_index in range(degree + 1):
            raw_columns.append(bell_curve * (tap_points / radius) ** power_index)
    orthonormal = []
    for column in raw_columns:
        vector = column.copy()
        for repeat_index in range(2):
            for earlier in orthonormal:
                vector = vector - np.dot(earlier, vector) * earlier
        orthonormal.append(vector / np.sqrt(np.dot(vector, vector)))
    return np.stack(orthonormal, axis=1).astype(np.float32)


def pair_layout():
    column_ids = []
    row_ids = []
    filter_runs = []
    offset = 0
    for degree in poly_degrees:
        for first_index in range(degree + 1):
            filter_runs.append((offset + first_index, offset, offset + degree - first_index + 1))
            for second_index in range(degree + 1 - first_index):
                column_ids.append(offset + first_index)
                row_ids.append(offset + second_index)
        offset += degree + 1
    return (column_ids, row_ids, filter_runs)


def band_tables(start_rows, patch_rows):
    values = filter_table(KR)
    taps_count = 2 * KR + 1
    row_band = np.zeros((NF, start_rows, patch_rows), np.float32)
    for start in range(start_rows):
        stop = min(start + taps_count, patch_rows)
        row_band[:, start, start:stop] = values.T[:, : stop - start]
    column_band = np.zeros((2 * LANES, NF, LANES), np.float32)
    for out_column in range(LANES):
        column_band[out_column : out_column + taps_count, :, out_column] = values
    return (
        jnp.asarray(row_band.astype(jnp.bfloat16)),
        jnp.asarray(column_band.reshape(2 * LANES, NF * LANES).astype(jnp.bfloat16)),
    )


def basis_runs():
    column_ids, row_ids, _ = pair_layout()
    index_of = {pair: k for k, pair in enumerate(zip(column_ids, row_ids))}
    runs = []
    offset = 0
    for degree in poly_degrees:
        for second in range(degree + 1):
            b = offset + second
            count = degree + 1 - second
            runs.append((b, offset, [index_of[(offset + i, b)] for i in range(count)]))
        offset += degree + 1
    return runs


def chunk_rows(group, per_tile):
    return -(-group * per_tile // 16) * 16


def peers_signal(barrier, axis, me, count):
    def one(i, carry):
        pl.semaphore_signal(
            barrier,
            inc=1,
            device_id={axis: lax.rem(me + 1 + i, count)},
            device_id_type=pl.DeviceIdType.MESH,
        )
        return carry

    lax.fori_loop(0, count - 1, one, 0)


def push(source, target, send_sem, recv_sem, axis, peer):
    return pltpu.make_async_remote_copy(
        src_ref=source,
        dst_ref=target,
        send_sem=send_sem,
        recv_sem=recv_sem,
        device_id={axis: peer},
        device_id_type=pl.DeviceIdType.MESH,
    )


def dispatch_kernel(
    patches,
    visit_parts,
    capacity,
    source_ref,
    live_ref,
    template_ref,
    science_ref,
    sigma_ref,
    details_ref,
    whole_ref,
    arrived_ref,
    arrived_details_ref,
    stage,
    packed,
    template_send,
    template_recv,
    tile_send,
    tile_recv,
    details_send,
    details_recv,
):
    me = lax.axis_index("patch")
    my_visit = lax.axis_index("visit")
    group = min(GROUP, capacity)
    chunk = chunk_rows(group, 4)
    peer_rows = capacity // group * chunk
    share = template_ref.shape[0]

    barrier = pltpu.get_barrier_semaphore()
    peers_signal(barrier, "patch", me, patches)
    peers_signal(barrier, "visit", my_visit, visit_parts)
    if chunk != 4 * group:
        stage[...] = jnp.zeros_like(stage)

    def template_rows(index):
        return whole_ref.at[pl.ds(pl.multiple_of(index * share, 16), share), :]

    def tile_rows(ref, index):
        return ref.at[pl.ds(pl.multiple_of(index * peer_rows, 16), peer_rows), :]

    template_rows(my_visit)[...] = template_ref[...].astype(jnp.bfloat16)
    arrived_details_ref[me] = details_ref[me]
    pl.semaphore_wait(barrier, patches - 1 + visit_parts - 1)

    def template_copy(peer, owner):
        return push(
            template_rows(owner),
            template_rows(owner),
            template_send.at[peer],
            template_recv.at[owner],
            "visit",
            peer,
        )

    def details_copy(peer, owner):
        return push(
            details_ref.at[peer],
            arrived_details_ref.at[owner],
            details_send.at[peer],
            details_recv.at[owner],
            "patch",
            peer,
        )

    def tile_copy(peer, owner):
        return push(
            tile_rows(packed, peer),
            tile_rows(arrived_ref, owner),
            tile_send.at[peer],
            tile_recv.at[owner],
            "patch",
            peer,
        )

    for i in range(1, visit_parts):
        template_copy(lax.rem(my_visit + i, visit_parts), my_visit).start()

    def pack(peer):
        def pack_group(q, carry):
            base = pl.multiple_of(peer * peer_rows + q * chunk, 16)
            for t in range(group):
                slot = peer * capacity + q * group + t
                tile = source_ref[slot]
                sigma = sigma_ref[tile] * live_ref[slot]
                stage[pl.ds(base + 4 * t, 2), :] = science_ref[tile] * sigma
                stage[pl.ds(base + 4 * t + 2, 2), :] = sigma
            return carry

        lax.fori_loop(0, capacity // group, pack_group, 0)
        rows = pl.ds(pl.multiple_of(peer * peer_rows, 16), peer_rows)
        return rows, stage[rows, :].astype(jnp.bfloat16)

    def pack_and_send(i, carry):
        peer = lax.rem(me + 1 + i, patches)
        details_copy(peer, me).start()
        rows, values = pack(peer)
        packed[rows, :] = values
        tile_copy(peer, me).start()
        return carry

    lax.fori_loop(0, patches - 1, pack_and_send, 0)
    rows, values = pack(me)
    arrived_ref[rows, :] = values

    for i in range(1, visit_parts):
        peer = lax.rem(my_visit + i, visit_parts)
        template_copy(peer, my_visit).wait_send()
        template_copy(peer, peer).wait_recv()

    def finish(i, carry):
        peer = lax.rem(me + 1 + i, patches)
        details_copy(peer, me).wait_send()
        tile_copy(peer, me).wait_send()
        details_copy(peer, peer).wait_recv()
        tile_copy(peer, peer).wait_recv()
        return carry

    lax.fori_loop(0, patches - 1, finish, 0)


def fit_kernel(
    capacity,
    visit_ref,
    row_ref,
    column_ref,
    template_ref,
    row_band_ref,
    column_band_ref,
    arrived_ref,
    gram_ref,
    picked_out,
    filtered,
    images,
    total,
    picked_all,
    picked_sems,
):
    start_rows = row_band_ref.shape[1]
    image_rows = images.shape[1] // ROWS
    patch_columns = template_ref.shape[1]
    blocks = patch_columns // LANES
    slot_count = picked_all.shape[0]
    group = min(GROUP, capacity)
    chunk = chunk_rows(group, 4)

    for b in range(NF):
        filtered[b, :, :patch_columns] = jnp.dot(
            row_band_ref[b], template_ref[...], preferred_element_type=jnp.float32
        ).astype(jnp.bfloat16)
        filtered[b, :, patch_columns:] = jnp.zeros((start_rows, LANES), jnp.bfloat16)

    def column_block(j, carry):
        at = pl.multiple_of(j * LANES, LANES)
        for b, first, indices in basis_runs():
            product = jnp.dot(
                filtered[b, :, pl.ds(at, 2 * LANES)],
                column_band_ref[:, first * LANES : (first + len(indices)) * LANES],
                preferred_element_type=jnp.float32,
            )
            for i, k in enumerate(indices):
                images[j, k * image_rows : k * image_rows + start_rows, :] = product[
                    :, i * LANES : (i + 1) * LANES
                ]
        return carry

    lax.fori_loop(0, blocks, column_block, 0)

    total[...] = jnp.zeros_like(total)
    lane = lax.broadcasted_iota(jnp.int32, (8, LANES), 1)
    eighth = lax.broadcasted_iota(jnp.int32, (8, LANES), 0)
    basis = lax.broadcasted_iota(jnp.int32, (ROWS, LANES), 0)
    part = lax.broadcasted_iota(jnp.int32, (ROWS, LANES), 1) // ROWS

    def pick(slot):
        column = column_ref[slot]
        block = column // LANES
        shift = column % LANES
        halves = []
        for i in range(2):
            pieces = []
            for k in range(0, ROWS, 8):
                rows = pl.ds(k * image_rows + row_ref[slot] + i, 8, stride=image_rows)
                piece = pltpu.roll(
                    jnp.where(lane >= shift, images[block, rows, :], images[block + 1, rows, :]),
                    (LANES - shift) % LANES,
                    axis=1,
                )
                if k + 8 >= NB:
                    constant = jnp.where(eighth + k == NB - 1, 1.0, 0.0)
                    piece = jnp.where(eighth + k < NB - 1, piece, constant)
                pieces.append(piece)
            halves.append(jnp.concatenate(pieces, axis=0))
        return halves

    def tile_group(g, carry):
        chunks = [
            arrived_ref[pl.ds(pl.multiple_of((g * (GROUP // group) + c) * chunk, 16), chunk), :]
            for c in range(GROUP // group)
        ]
        chunks = [values.astype(jnp.float32) for values in chunks]
        designs = []
        for t in range(GROUP):
            s = g * GROUP + t
            values = chunks[t // group][t % group * 4 : t % group * 4 + 4]
            halves = pick(s)
            for i in range(2):
                picked_all[s, i * ROWS : (i + 1) * ROWS, :] = halves[i]
            designs.append(
                jnp.concatenate(
                    [
                        jnp.where(
                            basis == RHS,
                            values[i : i + 1],
                            halves[i] * values[2 + i : 3 + i],
                        ).astype(jnp.bfloat16)
                        for i in range(2)
                    ],
                    axis=1,
                )
            )
        design = jnp.concatenate(designs, axis=0)
        products = lax.dot_general(
            design, design, (((1,), (1,)), ((), ())), preferred_element_type=jnp.float32
        )
        per = LANES // ROWS
        for t in range(GROUP):
            own = products[
                t * ROWS : (t + 1) * ROWS, (t // per) * LANES : (t // per + 1) * LANES
            ]
            total[visit_ref[g * GROUP + t]] += jnp.where(part == t % per, own, 0.0)
        return carry

    stages = picked_sems.shape[0]
    groups = slot_count // GROUP // stages
    copies = []
    for n in range(stages):
        lax.fori_loop(n * groups, (n + 1) * groups, tile_group, 0)
        rows = pl.ds(n * groups * GROUP, groups * GROUP)
        copies.append(
            pltpu.make_async_copy(picked_all.at[rows], picked_out.at[rows], picked_sems.at[n])
        )
        copies[-1].start()

    owners = gram_ref.shape[0]
    per_owner = VIS_DEV // owners
    for owner in range(owners):
        merged = jnp.zeros((ROWS, LANES), jnp.float32)
        for i in range(per_owner):
            folded = total[owner * per_owner + i]
            folded = folded + pltpu.roll(folded, 2 * ROWS, axis=1)
            folded = folded + pltpu.roll(folded, ROWS, axis=1)
            merged = jnp.where(part == i, folded, merged)
        gram_ref[owner] = merged
    for copy in copies:
        copy.wait()


def solve_systems(system):
    row_id = lax.broadcasted_iota(jnp.int32, system.shape, 1)
    column_id = lax.broadcasted_iota(jnp.int32, system.shape, 2)
    for p in range(NB):
        pivot_row = system[:, p : p + 1, :]
        inverse = 1.0 / system[:, p : p + 1, p : p + 1]
        factor = system[:, :, p : p + 1] * inverse
        system = jnp.where(row_id == p, system, system - factor * pivot_row)
    diagonal = jnp.sum(jnp.where(row_id == column_id, system, 0.0), axis=2, keepdims=True)
    solved = system[:, :, RHS : RHS + 1] / diagonal
    return jnp.where(row_id < NB, jnp.broadcast_to(solved, system.shape), 0.0)


def finish_kernel(
    patches,
    capacity,
    visit_ref,
    place_ref,
    gram_ref,
    picked_in,
    science_ref,
    difference_ref,
    coefficient_ref,
    picked,
    grams,
    solved,
    arrived_solved,
    stage,
    packed,
    returned,
    returned_wide,
    picked_sem,
    gram_send,
    gram_recv,
    solved_send,
    solved_recv,
    model_send,
    model_recv,
):
    me = lax.axis_index("patch")
    owners = gram_ref.shape[0]
    per_owner = VIS_DEV // owners
    group = min(GROUP, capacity)
    chunk = chunk_rows(group, 2)
    peer_rows = capacity // group * chunk
    load = pltpu.make_async_copy(picked_in, picked, picked_sem)
    load.start()
    barrier = pltpu.get_barrier_semaphore()
    peers_signal(barrier, "patch", me, patches)
    if chunk != 2 * group:
        stage[...] = jnp.zeros_like(stage)
    pl.semaphore_wait(barrier, patches - 1)

    def when_owner(index, action):
        if owners == patches:
            action()
        else:
            pl.when(index < owners)(action)

    def each_peer(action):
        def one(i, carry):
            action(lax.rem(me + 1 + i, patches))
            return carry

        lax.fori_loop(0, patches - 1, one, 0)

    def gram_copy(peer, sender):
        return push(
            gram_ref.at[peer], grams.at[sender], gram_send.at[peer], gram_recv.at[sender],
            "patch", peer,
        )

    def solved_copy(peer, sender):
        return push(
            solved, arrived_solved.at[sender], solved_send.at[peer], solved_recv.at[sender],
            "patch", peer,
        )

    def tile_rows(ref, index):
        return ref.at[pl.ds(pl.multiple_of(index * peer_rows, 16), peer_rows), :]

    def model_copy(peer, sender):
        return push(
            tile_rows(packed, peer), tile_rows(returned, sender), model_send.at[peer],
            model_recv.at[sender], "patch", peer,
        )

    each_peer(lambda peer: when_owner(peer, lambda: gram_copy(peer, me).start()))

    def solve_own():
        grams[me] = gram_ref[me]
        each_peer(lambda peer: gram_copy(lax.rem(me, owners), peer).wait_recv())
        summed = jnp.sum(grams[...], axis=0)
        systems = [summed] + [
            pltpu.roll(summed, LANES - i * ROWS, axis=1) for i in range(1, per_owner)
        ]
        values = solve_systems(jnp.stack(systems, axis=0))
        lane = lax.broadcasted_iota(jnp.int32, (ROWS, LANES), 1)
        merged = values[0]
        for i in range(1, per_owner):
            merged = jnp.where(lane == i, values[i], merged)
        solved[...] = merged
        arrived_solved[me] = merged
        each_peer(lambda peer: solved_copy(peer, me).start())

    when_owner(me, solve_own)
    each_peer(
        lambda peer: when_owner(peer, lambda: solved_copy(peer, peer).wait_recv())
    )
    for v in range(VIS_DEV):
        i = v % per_owner
        coefficient_ref[v] = jnp.broadcast_to(
            arrived_solved[v // per_owner][:, i : i + 1], (ROWS, LANES)
        )
    load.wait()

    def model_of(peer):
        def model_group(q, carry):
            base = pl.multiple_of(peer * peer_rows + q * chunk, 16)
            for t in range(group):
                s = peer * capacity + q * group + t
                values = coefficient_ref[visit_ref[s]]
                for i in range(2):
                    stage[pl.ds(base + 2 * t + i, 1), :] = jnp.sum(
                        picked[s, i * ROWS : (i + 1) * ROWS, :] * values, axis=0, keepdims=True
                    )
            return carry

        lax.fori_loop(0, capacity // group, model_group, 0)
        rows = pl.ds(pl.multiple_of(peer * peer_rows, 16), peer_rows)
        return rows, stage[rows, :].astype(jnp.bfloat16)

    def model_and_send(peer):
        rows, values = model_of(peer)
        packed[rows, :] = values
        model_copy(peer, me).start()

    each_peer(model_and_send)
    rows, values = model_of(me)
    returned[rows, :] = values

    def finish(peer):
        when_owner(peer, lambda: gram_copy(peer, me).wait_send())
        when_owner(me, lambda: solved_copy(peer, me).wait_send())
        model_copy(peer, me).wait_send()
        model_copy(peer, peer).wait_recv()

    each_peer(finish)
    returned_wide[...] = returned[...].astype(jnp.float32)

    def subtract(q, carry):
        for t in range(GROUP):
            tile = q * GROUP + t
            difference_ref[tile] = science_ref[tile] - returned_wide[pl.ds(place_ref[tile], 2), :]
        return carry

    lax.fori_loop(0, science_ref.shape[0] // GROUP, subtract, 0)


def per_device(science, inverse_sigma, template, destination, offsets, visit_local):
    patches = lax.axis_size("patch")
    visit_parts = lax.axis_size("visit")
    tile_count, row_count, column_count = science.shape
    capacity = max(2, 2 * tile_count // patches)
    slot_count = patches * capacity
    patch_rows, patch_columns = template.shape[1] * visit_parts, template.shape[2]
    start_rows = -(-(patch_rows - 2 * KR) // 16) * 16
    image_rows = start_rows + 8
    row_band, column_band = band_tables(start_rows, patch_rows)
    order_ids = jnp.arange(tile_count, dtype=jnp.int32)
    same_patch = destination[:, None] == destination[None, :]
    before = order_ids[None, :] < order_ids[:, None]
    tile_rank = jnp.sum(jnp.where(same_patch & before, 1, 0), axis=1).astype(jnp.int32)
    slot_of_tile = destination * capacity + tile_rank
    slot_ids = jnp.arange(slot_count, dtype=jnp.int32)
    holds = slot_of_tile[None, :] == slot_ids[:, None]
    routed = jnp.stack(
        [jnp.ones_like(order_ids), order_ids, visit_local, offsets[:, 0], offsets[:, 1]], axis=0
    )
    routed = jnp.sum(jnp.where(holds[None], routed[:, None, :], 0), axis=2)
    details = jnp.pad(
        routed[2:].reshape(3, patches, capacity).transpose(1, 0, 2),
        ((0, 0), (0, 5), (0, LANES - capacity)),
    )
    group = min(GROUP, capacity)
    tile_chunk = chunk_rows(group, 4)
    tile_total = slot_count // group * tile_chunk
    model_chunk = chunk_rows(group, 2)
    model_total = slot_count // group * model_chunk
    place_of_tile = slot_of_tile // group * model_chunk + slot_of_tile % group * 2

    smem = pl.BlockSpec(memory_space=pltpu.SMEM)
    vmem = pl.BlockSpec(memory_space=pltpu.VMEM)
    anywhere = pl.BlockSpec(memory_space=pl.ANY)
    dma = pltpu.SemaphoreType.DMA
    whole_template, arrived, arrived_details = pl.pallas_call(
        functools.partial(dispatch_kernel, patches, visit_parts, capacity),
        out_shape=(
            jax.ShapeDtypeStruct((patch_rows, patch_columns), jnp.bfloat16),
            jax.ShapeDtypeStruct((tile_total, LANES), jnp.bfloat16),
            jax.ShapeDtypeStruct((patches, 8, LANES), jnp.int32),
        ),
        in_specs=[smem] * 2 + [vmem] * 4,
        out_specs=(vmem,) * 3,
        scratch_shapes=[
            pltpu.VMEM((tile_total, LANES), jnp.float32),
            pltpu.VMEM((tile_total, LANES), jnp.bfloat16),
            dma((visit_parts,)),
            dma((visit_parts,)),
        ]
        + [dma((patches,))] * 4,
        compiler_params=pltpu.CompilerParams(
            vmem_limit_bytes=VMEM_BYTES, collective_id=0, has_side_effects=True
        ),
    )(
        routed[1],
        routed[0].astype(jnp.float32),
        template[0],
        science,
        inverse_sigma,
        details,
    )
    arrived_details = arrived_details[:, :3, :capacity].transpose(1, 0, 2).reshape(3, slot_count)
    visits = arrived_details[0]
    owners = min(patches, VIS_DEV)
    picked_shape = (slot_count, row_count * ROWS, LANES)
    gram, picked = pl.pallas_call(
        functools.partial(fit_kernel, capacity),
        out_shape=(
            jax.ShapeDtypeStruct((owners, ROWS, LANES), jnp.float32),
            jax.ShapeDtypeStruct(picked_shape, jnp.float32),
        ),
        in_specs=[smem] * 3 + [vmem] * 4,
        out_specs=(vmem, anywhere),
        scratch_shapes=[
            pltpu.VMEM((NF, start_rows, patch_columns + LANES), jnp.bfloat16),
            pltpu.VMEM((patch_columns // LANES, image_rows * ROWS, LANES), jnp.float32),
            pltpu.VMEM((VIS_DEV, ROWS, LANES), jnp.float32),
            pltpu.VMEM(picked_shape, jnp.float32),
            dma((4,)),
        ],
        compiler_params=pltpu.CompilerParams(vmem_limit_bytes=VMEM_BYTES),
    )(
        visits,
        arrived_details[1],
        arrived_details[2],
        whole_template,
        row_band,
        column_band,
        arrived,
    )
    difference, solved = pl.pallas_call(
        functools.partial(finish_kernel, patches, capacity),
        out_shape=(
            jax.ShapeDtypeStruct(science.shape, jnp.float32),
            jax.ShapeDtypeStruct((VIS_DEV, ROWS, LANES), jnp.float32),
        ),
        in_specs=[smem] * 2 + [vmem, anywhere, vmem],
        out_specs=(vmem, vmem),
        scratch_shapes=[
            pltpu.VMEM(picked_shape, jnp.float32),
            pltpu.VMEM((patches, ROWS, LANES), jnp.float32),
            pltpu.VMEM((ROWS, LANES), jnp.float32),
            pltpu.VMEM((owners, ROWS, LANES), jnp.float32),
            pltpu.VMEM((model_total, LANES), jnp.float32),
            pltpu.VMEM((model_total, LANES), jnp.bfloat16),
            pltpu.VMEM((model_total, LANES), jnp.bfloat16),
            pltpu.VMEM((model_total, LANES), jnp.float32),
            dma,
            dma((owners,)),
            dma((patches,)),
            dma((patches,)),
            dma((owners,)),
            dma((patches,)),
            dma((patches,)),
        ],
        compiler_params=pltpu.CompilerParams(
            vmem_limit_bytes=VMEM_BYTES, collective_id=1, has_side_effects=True
        ),
    )(visits, place_of_tile, gram, picked, science)
    return (difference, solved[:, :NB, 0])


def solution(mesh):
    return jax.shard_map(
        per_device,
        mesh=mesh,
        in_specs=(
            P(("patch", "visit"), None, None),
            P(("patch", "visit"), None, None),
            P("patch", "visit", None),
            P(("patch", "visit")),
            P(("patch", "visit"), None),
            P(("patch", "visit")),
        ),
        out_specs=(P(("patch", "visit"), None, None), P("visit", None)),
        check_vma=False,
    )
```

```python
import functools

import jax
import jax.numpy as jnp
import numpy as np
from jax import lax
from jax.experimental import pallas as pl
from jax.experimental.pallas import tpu as pltpu
from jax.sharding import PartitionSpec as P

KR = 10
NF = 11
NB = 28
VIS_DEV = 16
ROWS = 32
RHS = NB
GROUP = 8
LANES = 128
VMEM_BYTES = 60 * 1024 * 1024


gauss_widths = (1.0, 2.0, 4.0)
poly_degrees = (4, 2, 2)


def filter_table(radius):
    tap_points = np.arange(-radius, radius + 1) * 1.0
    raw_columns = []
    for width_value, degree in zip(gauss_widths, poly_degrees):
        bell_curve = np.exp(-tap_points * tap_points / (2.0 * width_value * width_value))
        for power_index in range(degree + 1):
            raw_columns.append(bell_curve * (tap_points / radius) ** power_index)
    orthonormal = []
    for column in raw_columns:
        vector = column.copy()
        for repeat_index in range(2):
            for earlier in orthonormal:
                vector = vector - np.dot(earlier, vector) * earlier
        orthonormal.append(vector / np.sqrt(np.dot(vector, vector)))
    return np.stack(orthonormal, axis=1).astype(np.float32)


def pair_layout():
    column_ids = []
    row_ids = []
    filter_runs = []
    offset = 0
    for degree in poly_degrees:
        for first_index in range(degree + 1):
            filter_runs.append((offset + first_index, offset, offset + degree - first_index + 1))
            for second_index in range(degree + 1 - first_index):
                column_ids.append(offset + first_index)
                row_ids.append(offset + second_index)
        offset += degree + 1
    return (column_ids, row_ids, filter_runs)


def band_tables(start_rows, patch_rows):
    values = filter_table(KR)
    taps_count = 2 * KR + 1
    row_band = np.zeros((NF, start_rows, patch_rows), np.float32)
    for start in range(start_rows):
        stop = min(start + taps_count, patch_rows)
        row_band[:, start, start:stop] = values.T[:, : stop - start]
    column_band = np.zeros((2 * LANES, NF, LANES), np.float32)
    for out_column in range(LANES):
        column_band[out_column : out_column + taps_count, :, out_column] = values
    return (
        jnp.asarray(row_band.astype(jnp.bfloat16)),
        jnp.asarray(column_band.reshape(2 * LANES, NF * LANES).astype(jnp.bfloat16)),
    )


def basis_runs():
    column_ids, row_ids, _ = pair_layout()
    index_of = {pair: k for k, pair in enumerate(zip(column_ids, row_ids))}
    runs = []
    offset = 0
    for degree in poly_degrees:
        for second in range(degree + 1):
            b = offset + second
            count = degree + 1 - second
            runs.append((b, offset, [index_of[(offset + i, b)] for i in range(count)]))
        offset += degree + 1
    return runs


def chunk_rows(group, per_tile):
    return -(-group * per_tile // 16) * 16


def peers_signal(barrier, axis, me, count):
    def one(i, carry):
        pl.semaphore_signal(
            barrier,
            inc=1,
            device_id={axis: lax.rem(me + 1 + i, count)},
            device_id_type=pl.DeviceIdType.MESH,
        )
        return carry

    lax.fori_loop(0, count - 1, one, 0)


def push(source, target, send_sem, recv_sem, axis, peer):
    return pltpu.make_async_remote_copy(
        src_ref=source,
        dst_ref=target,
        send_sem=send_sem,
        recv_sem=recv_sem,
        device_id={axis: peer},
        device_id_type=pl.DeviceIdType.MESH,
    )


def solve_systems(system):
    row_id = lax.broadcasted_iota(jnp.int32, system.shape, 1)
    column_id = lax.broadcasted_iota(jnp.int32, system.shape, 2)
    for p in range(NB):
        pivot_row = system[:, p : p + 1, :]
        inverse = 1.0 / system[:, p : p + 1, p : p + 1]
        factor = system[:, :, p : p + 1] * inverse
        system = jnp.where(row_id == p, system, system - factor * pivot_row)
    diagonal = jnp.sum(jnp.where(row_id == column_id, system, 0.0), axis=2, keepdims=True)
    solved = system[:, :, RHS : RHS + 1] / diagonal
    return jnp.where(row_id < NB, jnp.broadcast_to(solved, system.shape), 0.0)


def image_kernel(
    patches,
    visit_parts,
    capacity,
    place_ref,
    template_ref,
    science_ref,
    sigma_ref,
    details_ref,
    row_band_ref,
    column_band_ref,
    model_ref,
    coefficient_ref,
    whole,
    arrived,
    arrived_details,
    routes,
    stage,
    packed,
    filtered,
    images,
    picked,
    running,
    gram,
    grams,
    solved,
    arrived_solved,
    spread,
    model_packed,
    returned,
    routes_sem,
    template_send,
    template_recv,
    tile_send,
    tile_recv,
    details_send,
    details_recv,
    gram_send,
    gram_recv,
    solved_send,
    solved_recv,
    model_send,
    model_recv,
):
    me = lax.axis_index("patch")
    my_visit = lax.axis_index("visit")
    slot_count = patches * capacity
    group = min(GROUP, capacity)
    tile_chunk = chunk_rows(group, 4)
    tile_peer = capacity // group * tile_chunk
    model_chunk = chunk_rows(group, 2)
    model_peer = capacity // group * model_chunk
    share, patch_columns = template_ref.shape
    start_rows = row_band_ref.shape[1]
    image_rows = images.shape[1] // ROWS
    owners = gram.shape[0]
    per_owner = VIS_DEV // owners

    def rows_of(index, count):
        return pl.ds(pl.multiple_of(index * count, 16), count)

    def each_peer(action):
        def one(i, carry):
            action(lax.rem(me + 1 + i, patches))
            return carry

        lax.fori_loop(0, patches - 1, one, 0)

    def when_owner(index, action):
        if owners == patches:
            action()
        else:
            pl.when(index < owners)(action)

    def template_copy(peer, owner):
        rows = whole.at[rows_of(owner, share), :]
        return push(rows, rows, template_send.at[peer], template_recv.at[owner], "visit", peer)

    def patch_copy(source, target, send, recv, peer, sender):
        return push(source, target, send.at[peer], recv.at[sender], "patch", peer)

    def details_copy(peer, sender):
        return patch_copy(
            details_ref.at[peer], arrived_details.at[sender], details_send, details_recv, peer, sender
        )

    def tile_copy(peer, sender):
        return patch_copy(
            packed.at[rows_of(peer, tile_peer), :],
            arrived.at[rows_of(sender, tile_peer), :],
            tile_send,
            tile_recv,
            peer,
            sender,
        )

    def gram_copy(peer, sender):
        return patch_copy(gram.at[peer], grams.at[sender], gram_send, gram_recv, peer, sender)

    def solved_copy(peer, sender):
        return patch_copy(
            solved, arrived_solved.at[sender], solved_send, solved_recv, peer, sender
        )

    def model_copy(peer, sender):
        return patch_copy(
            model_packed.at[rows_of(peer, model_peer), :],
            returned.at[rows_of(sender, model_peer), :],
            model_send,
            model_recv,
            peer,
            sender,
        )

    def pack(peer):
        for n in range(capacity):
            tile = routes[peer, 5, n]
            sigma = sigma_ref[tile] * routes[peer, 6, n].astype(jnp.float32)
            at = peer * tile_peer + n // group * tile_chunk + n % group * 4
            stage[pl.ds(at, 2), :] = science_ref[tile] * sigma
            stage[pl.ds(at + 2, 2), :] = sigma
        return stage[rows_of(peer, tile_peer), :].astype(jnp.bfloat16)

    barrier = pltpu.get_barrier_semaphore()
    peers_signal(barrier, "patch", me, patches)
    peers_signal(barrier, "visit", my_visit, visit_parts)
    own_scalars = pltpu.make_async_copy(details_ref, routes, routes_sem.at[0])
    own_scalars.start()
    if tile_chunk != 4 * group:
        stage[...] = jnp.zeros_like(stage)
    whole[rows_of(my_visit, share), :] = template_ref[...].astype(jnp.bfloat16)
    arrived_details[me] = details_ref[me]
    running[slot_count] = jnp.zeros((ROWS, LANES), jnp.float32)
    filtered[:, :, patch_columns:] = jnp.zeros((NF, start_rows, LANES), jnp.bfloat16)
    own_scalars.wait()
    arrived[rows_of(me, tile_peer), :] = pack(me)
    pl.semaphore_wait(barrier, patches - 1 + visit_parts - 1)

    for i in range(1, visit_parts):
        template_copy(lax.rem(my_visit + i, visit_parts), my_visit).start()

    def pack_and_send(peer):
        details_copy(peer, me).start()
        packed[rows_of(peer, tile_peer), :] = pack(peer)
        tile_copy(peer, me).start()

    each_peer(pack_and_send)
    for i in range(1, visit_parts):
        peer = lax.rem(my_visit + i, visit_parts)
        template_copy(peer, peer).wait_recv()

    for b in range(NF):
        filtered[b, :, :patch_columns] = jnp.dot(
            row_band_ref[b], whole[...], preferred_element_type=jnp.float32
        ).astype(jnp.bfloat16)

    def column_block(j, carry):
        at = pl.multiple_of(j * LANES, LANES)
        for b, first, indices in basis_runs():
            product = jnp.dot(
                filtered[b, :, pl.ds(at, 2 * LANES)],
                column_band_ref[:, first * LANES : (first + len(indices)) * LANES],
                preferred_element_type=jnp.float32,
            )
            for i, k in enumerate(indices):
                images[j, k * image_rows : k * image_rows + start_rows, :] = product[
                    :, i * LANES : (i + 1) * LANES
                ]
        return carry

    lax.fori_loop(0, patch_columns // LANES, column_block, 0)

    each_peer(lambda peer: details_copy(peer, peer).wait_recv())
    to_scalars = pltpu.make_async_copy(arrived_details, routes, routes_sem.at[1])
    to_scalars.start()
    to_scalars.wait()
    each_peer(lambda peer: tile_copy(peer, peer).wait_recv())

    lane = lax.broadcasted_iota(jnp.int32, (8, LANES), 1)
    eighth = lax.broadcasted_iota(jnp.int32, (8, LANES), 0)
    basis = lax.broadcasted_iota(jnp.int32, (ROWS, LANES), 0)
    part = lax.broadcasted_iota(jnp.int32, (ROWS, LANES), 1) // ROWS

    def pick(row, column):
        block = column // LANES
        shift = column % LANES
        halves = []
        for i in range(2):
            pieces = []
            for k in range(0, ROWS, 8):
                rows = pl.ds(k * image_rows + row + i, 8, stride=image_rows)
                piece = pltpu.roll(
                    jnp.where(lane >= shift, images[block, rows, :], images[block + 1, rows, :]),
                    (LANES - shift) % LANES,
                    axis=1,
                )
                if k + 8 >= NB:
                    constant = jnp.where(eighth + k == NB - 1, 1.0, 0.0)
                    piece = jnp.where(eighth + k < NB - 1, piece, constant)
                pieces.append(piece)
            halves.append(jnp.concatenate(pieces, axis=0))
        return halves

    def tile_group(g, carry):
        chunks = [
            arrived[rows_of(g * (GROUP // group) + c, tile_chunk), :].astype(jnp.float32)
            for c in range(GROUP // group)
        ]
        designs = []
        flags = []
        for t in range(GROUP):
            s = g * GROUP + t
            sender, n = s // capacity, s % capacity
            values = chunks[t // group][t % group * 4 : t % group * 4 + 4]
            halves = pick(routes[sender, 1, n], routes[sender, 2, n])
            flags.append(routes[sender, 4, n].astype(jnp.float32))
            for i in range(2):
                picked[s, i * ROWS : (i + 1) * ROWS, :] = halves[i]
            designs.append(
                jnp.concatenate(
                    [
                        jnp.where(
                            basis == RHS,
                            values[i : i + 1],
                            halves[i] * values[2 + i : 3 + i],
                        ).astype(jnp.bfloat16)
                        for i in range(2)
                    ],
                    axis=1,
                )
            )
        design = jnp.concatenate(designs, axis=0)
        products = lax.dot_general(
            design, design, (((1,), (1,)), ((), ())), preferred_element_type=jnp.float32
        )
        per = LANES // ROWS
        for t in range(GROUP):
            own = products[
                t * ROWS : (t + 1) * ROWS, (t // per) * LANES : (t // per + 1) * LANES
            ]
            carry = carry * flags[t] + jnp.where(part == t % per, own, 0.0)
            running[g * GROUP + t] = carry
        return carry

    def two_groups(h, carry):
        return tile_group(2 * h + 1, tile_group(2 * h, carry))

    lax.fori_loop(
        0, slot_count // GROUP // 2, two_groups, jnp.zeros((ROWS, LANES), jnp.float32)
    )

    def gram_of(owner):
        merged = jnp.zeros((ROWS, LANES), jnp.float32)
        for i in range(per_owner):
            v = owner * per_owner + i
            if patches <= VIS_DEV:
                folded = running[routes[0, 3, v]]
                for sender in range(1, patches):
                    folded = folded + running[routes[sender, 3, v]]
            else:
                folded = lax.fori_loop(
                    0,
                    patches,
                    lambda sender, sums: sums + running[routes[sender, 3, v]],
                    jnp.zeros((ROWS, LANES), jnp.float32),
                )
            folded = folded + pltpu.roll(folded, 2 * ROWS, axis=1)
            folded = folded + pltpu.roll(folded, ROWS, axis=1)
            merged = jnp.where(part == i, folded, merged)
        return merged

    def gram_and_send(peer):
        gram[peer] = gram_of(peer)
        gram_copy(peer, me).start()

    each_peer(lambda peer: when_owner(peer, lambda: gram_and_send(peer)))

    def solve_own():
        grams[me] = gram_of(me)
        each_peer(lambda peer: gram_copy(lax.rem(me, owners), peer).wait_recv())
        summed = jnp.sum(grams[...], axis=0)
        systems = [summed] + [
            pltpu.roll(summed, LANES - i * ROWS, axis=1) for i in range(1, per_owner)
        ]
        values = solve_systems(jnp.stack(systems, axis=0))
        merged = values[0]
        for i in range(1, per_owner):
            merged = jnp.where(
                lax.broadcasted_iota(jnp.int32, (ROWS, LANES), 1) == i, values[i], merged
            )
        solved[...] = merged
        arrived_solved[me] = merged
        each_peer(lambda peer: solved_copy(peer, me).start())

    when_owner(me, solve_own)
    each_peer(lambda peer: when_owner(peer, lambda: solved_copy(peer, peer).wait_recv()))
    for v in range(VIS_DEV):
        i = v % per_owner
        spread[v] = jnp.broadcast_to(arrived_solved[v // per_owner][:, i : i + 1], (ROWS, LANES))

    def model_of(peer):
        for n in range(capacity):
            s = peer * capacity + n
            values = spread[routes[peer, 0, n]]
            at = peer * model_peer + n // group * model_chunk + n % group * 2
            for i in range(2):
                stage[pl.ds(at + i, 1), :] = jnp.sum(
                    picked[s, i * ROWS : (i + 1) * ROWS, :] * values, axis=0, keepdims=True
                )
        return stage[rows_of(peer, model_peer), :].astype(jnp.bfloat16)

    def model_and_send(peer):
        model_packed[rows_of(peer, model_peer), :] = model_of(peer)
        model_copy(peer, me).start()

    each_peer(model_and_send)
    returned[rows_of(me, model_peer), :] = model_of(me)
    diagonal = basis == lax.broadcasted_iota(jnp.int32, (ROWS, LANES), 1)
    for v in range(VIS_DEV):
        coefficient_ref[v : v + 1, :] = jnp.sum(
            jnp.where(diagonal, spread[v], 0.0), axis=0, keepdims=True
        )

    for i in range(1, visit_parts):
        template_copy(lax.rem(my_visit + i, visit_parts), my_visit).wait_send()

    def finish(peer):
        details_copy(peer, me).wait_send()
        tile_copy(peer, me).wait_send()
        when_owner(peer, lambda: gram_copy(peer, me).wait_send())
        when_owner(me, lambda: solved_copy(peer, me).wait_send())
        model_copy(peer, me).wait_send()
        model_copy(peer, peer).wait_recv()

    each_peer(finish)
    stage[: returned.shape[0], :] = returned[...].astype(jnp.float32)

    def give_back(q, carry):
        for t in range(2 * GROUP):
            tile = q * 2 * GROUP + t
            model_ref[tile] = stage[pl.ds(place_ref[tile], 2), :]
        return carry

    lax.fori_loop(0, model_ref.shape[0] // (2 * GROUP), give_back, 0)


def per_device(science, inverse_sigma, template, destination, offsets, visit_local):
    patches = lax.axis_size("patch")
    visit_parts = lax.axis_size("visit")
    tile_count, row_count, column_count = science.shape
    capacity = max(2, 2 * tile_count // patches)
    slot_count = patches * capacity
    patch_rows, patch_columns = template.shape[1] * visit_parts, template.shape[2]
    start_rows = -(-(patch_rows - 2 * KR) // 16) * 16
    image_rows = start_rows + 8
    row_band, column_band = band_tables(start_rows, patch_rows)
    order_ids = jnp.arange(tile_count, dtype=jnp.int32)
    sort_key = visit_local * tile_count + order_ids
    same_patch = destination[:, None] == destination[None, :]
    same_visit = visit_local[:, None] == visit_local[None, :]
    tile_rank = jnp.sum(
        jnp.where(same_patch & (sort_key[None, :] < sort_key[:, None]), 1, 0), axis=1
    ).astype(jnp.int32)
    continues = jnp.any(
        same_patch & same_visit & (order_ids[None, :] < order_ids[:, None]), axis=1
    ).astype(jnp.int32)
    slot_of_tile = destination * capacity + tile_rank
    slot_ids = jnp.arange(slot_count, dtype=jnp.int32)
    holds = slot_of_tile[None, :] == slot_ids[:, None]
    per_slot = jnp.stack(
        [
            visit_local,
            offsets[:, 0],
            offsets[:, 1],
            continues,
            order_ids,
            jnp.ones_like(order_ids),
        ],
        axis=0,
    )
    per_slot = jnp.sum(jnp.where(holds[None], per_slot[:, None, :], 0), axis=2)
    per_slot = per_slot.reshape(6, patches, capacity).transpose(1, 0, 2)
    per_slot = jnp.pad(per_slot, ((0, 0), (0, 0), (0, LANES - capacity)))
    in_patch = destination[None, :] == jnp.arange(patches, dtype=jnp.int32)[:, None]
    visit_ids = jnp.arange(VIS_DEV, dtype=jnp.int32)[None, :, None]
    up_to = jnp.sum(jnp.where(in_patch[:, None] & (visit_local <= visit_ids), 1, 0), axis=2)
    present = jnp.any(in_patch[:, None] & (visit_local == visit_ids), axis=2)
    last = jnp.where(present, lax.axis_index("patch") * capacity + up_to - 1, slot_count)
    last = jnp.pad(last, ((0, 0), (0, LANES - VIS_DEV)))
    details = jnp.concatenate(
        [per_slot[:, :3], last[:, None], per_slot[:, 3:], jnp.zeros_like(last)[:, None]], axis=1
    ).astype(jnp.int32)
    group = min(GROUP, capacity)
    tile_total = slot_count // group * chunk_rows(group, 4)
    model_chunk = chunk_rows(group, 2)
    model_total = slot_count // group * model_chunk
    place_of_tile = slot_of_tile // group * model_chunk + slot_of_tile % group * 2

    owners = min(patches, VIS_DEV)
    smem = pl.BlockSpec(memory_space=pltpu.SMEM)
    vmem = pl.BlockSpec(memory_space=pltpu.VMEM)
    dma = pltpu.SemaphoreType.DMA
    wide, half = jnp.float32, jnp.bfloat16
    own_model, coefficients = pl.pallas_call(
        functools.partial(image_kernel, patches, visit_parts, capacity),
        out_shape=(
            jax.ShapeDtypeStruct(science.shape, wide),
            jax.ShapeDtypeStruct((VIS_DEV, LANES), wide),
        ),
        in_specs=[smem] + [vmem] * 6,
        out_specs=(vmem, vmem),
        scratch_shapes=[
            pltpu.VMEM((patch_rows, patch_columns), half),
            pltpu.VMEM((tile_total, LANES), half),
            pltpu.VMEM((patches, 8, LANES), jnp.int32),
            pltpu.SMEM((patches, 8, LANES), jnp.int32),
            pltpu.VMEM((tile_total, LANES), wide),
            pltpu.VMEM((tile_total, LANES), half),
            pltpu.VMEM((NF, start_rows, patch_columns + LANES), half),
            pltpu.VMEM((patch_columns // LANES, image_rows * ROWS, LANES), wide),
            pltpu.VMEM((slot_count, row_count * ROWS, LANES), wide),
            pltpu.VMEM((slot_count + 1, ROWS, LANES), wide),
            pltpu.VMEM((owners, ROWS, LANES), wide),
            pltpu.VMEM((patches, ROWS, LANES), wide),
            pltpu.VMEM((ROWS, LANES), wide),
            pltpu.VMEM((owners, ROWS, LANES), wide),
            pltpu.VMEM((VIS_DEV, ROWS, LANES), wide),
            pltpu.VMEM((model_total, LANES), half),
            pltpu.VMEM((model_total, LANES), half),
            dma((2,)),
            dma((visit_parts,)),
            dma((visit_parts,)),
            dma((patches,)),
            dma((patches,)),
            dma((patches,)),
            dma((patches,)),
            dma((owners,)),
            dma((patches,)),
            dma((patches,)),
            dma((owners,)),
            dma((patches,)),
            dma((patches,)),
        ],
        compiler_params=pltpu.CompilerParams(
            vmem_limit_bytes=VMEM_BYTES, collective_id=0, has_side_effects=True
        ),
    )(
        place_of_tile,
        template[0],
        science,
        inverse_sigma,
        details,
        row_band,
        column_band,
    )
    return (science - own_model, coefficients[:, :NB])


def solution(mesh):
    return jax.shard_map(
        per_device,
        mesh=mesh,
        in_specs=(
            P(("patch", "visit"), None, None),
            P(("patch", "visit"), None, None),
            P("patch", "visit", None),
            P(("patch", "visit")),
            P(("patch", "visit"), None),
            P(("patch", "visit")),
        ),
        out_specs=(P(("patch", "visit"), None, None), P("visit", None)),
        check_vma=False,
    )
```

```python
import functools

import jax
import jax.numpy as jnp
import numpy as np
from jax import lax
from jax.experimental import pallas as pl
from jax.experimental.pallas import tpu as pltpu
from jax.sharding import PartitionSpec as P

KR = 10
NF = 11
NB = 28
VIS_DEV = 16
ROWS = 32
RHS = NB
GROUP = 8
LANES = 128
VMEM_BYTES = 60 * 1024 * 1024


gauss_widths = (1.0, 2.0, 4.0)
poly_degrees = (4, 2, 2)


def filter_table(radius):
    tap_points = np.arange(-radius, radius + 1) * 1.0
    raw_columns = []
    for width_value, degree in zip(gauss_widths, poly_degrees):
        bell_curve = np.exp(-tap_points * tap_points / (2.0 * width_value * width_value))
        for power_index in range(degree + 1):
            raw_columns.append(bell_curve * (tap_points / radius) ** power_index)
    orthonormal = []
    for column in raw_columns:
        vector = column.copy()
        for repeat_index in range(2):
            for earlier in orthonormal:
                vector = vector - np.dot(earlier, vector) * earlier
        orthonormal.append(vector / np.sqrt(np.dot(vector, vector)))
    return np.stack(orthonormal, axis=1).astype(np.float32)


def pair_layout():
    column_ids = []
    row_ids = []
    filter_runs = []
    offset = 0
    for degree in poly_degrees:
        for first_index in range(degree + 1):
            filter_runs.append((offset + first_index, offset, offset + degree - first_index + 1))
            for second_index in range(degree + 1 - first_index):
                column_ids.append(offset + first_index)
                row_ids.append(offset + second_index)
        offset += degree + 1
    return (column_ids, row_ids, filter_runs)


def band_tables(start_rows, patch_rows):
    values = filter_table(KR)
    taps_count = 2 * KR + 1
    row_band = np.zeros((NF, start_rows, patch_rows), np.float32)
    for start in range(start_rows):
        stop = min(start + taps_count, patch_rows)
        row_band[:, start, start:stop] = values.T[:, : stop - start]
    column_band = np.zeros((2 * LANES, NF, LANES), np.float32)
    for out_column in range(LANES):
        column_band[out_column : out_column + taps_count, :, out_column] = values
    return (
        jnp.asarray(row_band.astype(jnp.bfloat16)),
        jnp.asarray(column_band.reshape(2 * LANES, NF * LANES).astype(jnp.bfloat16)),
    )


def basis_runs():
    column_ids, row_ids, _ = pair_layout()
    index_of = {pair: k for k, pair in enumerate(zip(column_ids, row_ids))}
    runs = []
    offset = 0
    for degree in poly_degrees:
        for second in range(degree + 1):
            b = offset + second
            count = degree + 1 - second
            runs.append((b, offset, [index_of[(offset + i, b)] for i in range(count)]))
        offset += degree + 1
    return runs


def chunk_rows(group, per_tile):
    return -(-group * per_tile // 16) * 16


def peers_signal(barrier, axis, me, count):
    def one(i, carry):
        pl.semaphore_signal(
            barrier,
            inc=1,
            device_id={axis: lax.rem(me + 1 + i, count)},
            device_id_type=pl.DeviceIdType.MESH,
        )
        return carry

    lax.fori_loop(0, count - 1, one, 0)


def push(source, target, send_sem, recv_sem, axis, peer):
    return pltpu.make_async_remote_copy(
        src_ref=source,
        dst_ref=target,
        send_sem=send_sem,
        recv_sem=recv_sem,
        device_id={axis: peer},
        device_id_type=pl.DeviceIdType.MESH,
    )


def solve_systems(system):
    row_id = lax.broadcasted_iota(jnp.int32, system.shape, 1)
    column_id = lax.broadcasted_iota(jnp.int32, system.shape, 2)
    for p in range(NB):
        pivot_row = system[:, p : p + 1, :]
        inverse = 1.0 / system[:, p : p + 1, p : p + 1]
        factor = system[:, :, p : p + 1] * inverse
        system = jnp.where(row_id == p, system, system - factor * pivot_row)
    diagonal = jnp.sum(jnp.where(row_id == column_id, system, 0.0), axis=2, keepdims=True)
    solved = system[:, :, RHS : RHS + 1] / diagonal
    return jnp.where(row_id < NB, jnp.broadcast_to(solved, system.shape), 0.0)


def make_routes(
    patches, capacity, me, destination_ref, visit_ref, offsets_ref, details_ref, local_ref
):
    square = (LANES, LANES)
    lane = lax.broadcasted_iota(jnp.int32, square, 1)
    diagonal = lax.broadcasted_iota(jnp.int32, square, 0) == lane
    lane_row = lane[:1]
    slot_count = patches * capacity
    group = min(GROUP, capacity)
    chunk = chunk_rows(group, 2)

    def column(row):
        return jnp.sum(jnp.where(diagonal, row, 0), axis=1, keepdims=True)

    destination = destination_ref[...]
    key = (destination * VIS_DEV + visit_ref[...]) * LANES + lane_row
    key_column = column(key)
    pair_column = key_column // LANES
    patch_column = key_column // (LANES * VIS_DEV)
    earlier = (patch_column == destination) & (key_column < key)
    slot = destination * capacity + jnp.sum(jnp.where(earlier, 1, 0), axis=0, keepdims=True)
    slot_column = column(slot)
    rank_column = slot_column - patch_column * capacity
    values = [
        pair_column - patch_column * VIS_DEV,
        column(offsets_ref[0:1, :]),
        column(offsets_ref[1:2, :]),
        key_column - pair_column * LANES,
        jnp.ones((LANES, 1), jnp.int32),
    ]
    place = slot // group * chunk + slot % group * 2
    tables = []
    for block in range(slot_count // LANES):
        holds = slot_column == lane + block * LANES
        visit, row, col, order, live = [
            jnp.sum(jnp.where(holds, value, 0), axis=0, keepdims=True) for value in values
        ]
        follows = (visit == pltpu.roll(visit, 1, axis=1)) & (lane_row % capacity > 0) & (live > 0)
        tables.append([visit, row, col, jnp.where(follows, 1, 0)])
        local_ref[block] = jnp.concatenate(
            [visit, row, col, visit, visit, order, live, place], axis=0
        )
    for block in range(patches * VIS_DEV // LANES):
        found = jnp.max(
            jnp.where(pair_column == lane + block * LANES, rank_column, -1), axis=0, keepdims=True
        )
        last = jnp.where(
            found < 0, slot_count, jnp.minimum(found, capacity - 1) + me * capacity
        )
        for part in range(LANES // VIS_DEV):
            details_ref[block * (LANES // VIS_DEV) + part, 1:2, :] = (
                pltpu.roll(last, LANES - part * VIS_DEV, axis=1) if part else last
            )
    for patch in range(patches):
        table = tables[patch * capacity // LANES]
        merged = table[3]
        for q in range(4):
            shift = (q * capacity - patch * capacity) % LANES
            moved = pltpu.roll(table[q], shift, axis=1) if shift else table[q]
            merged = jnp.where(lane_row // capacity == q, moved, merged)
        details_ref[patch, 0:1, :] = merged


def image_kernel(
    patches,
    visit_parts,
    capacity,
    destination_ref,
    visit_ref,
    offsets_ref,
    template_ref,
    science_ref,
    sigma_ref,
    row_band_in,
    column_band_in,
    model_ref,
    coefficient_ref,
    whole,
    arrived,
    arrived_details,
    routes,
    details_ref,
    local_ref,
    local,
    row_band_ref,
    column_band_ref,
    stage,
    packed,
    filtered,
    images,
    picked,
    running,
    gram,
    grams,
    solved,
    arrived_solved,
    spread,
    model_packed,
    returned,
    routes_sem,
    band_sem,
    template_send,
    template_recv,
    tile_send,
    tile_recv,
    details_send,
    details_recv,
    gram_send,
    gram_recv,
    solved_send,
    solved_recv,
    model_send,
    model_recv,
):
    me = lax.axis_index("patch")
    my_visit = lax.axis_index("visit")
    slot_count = patches * capacity
    group = min(GROUP, capacity)
    tile_chunk = chunk_rows(group, 4)
    tile_peer = capacity // group * tile_chunk
    model_chunk = chunk_rows(group, 2)
    model_peer = capacity // group * model_chunk
    share, patch_columns = template_ref.shape
    start_rows = row_band_ref.shape[1]
    image_rows = images.shape[1] // ROWS
    owners = gram.shape[0]
    per_owner = VIS_DEV // owners

    def rows_of(index, count):
        return pl.ds(pl.multiple_of(index * count, 16), count)

    def each_peer(action):
        def one(i, carry):
            action(lax.rem(me + 1 + i, patches))
            return carry

        lax.fori_loop(0, patches - 1, one, 0)

    def when_owner(index, action):
        if owners == patches:
            action()
        else:
            pl.when(index < owners)(action)

    near = my_visit + 1 - 2 * lax.rem(my_visit, 2)
    far = lax.rem(my_visit + 2, 4)

    def template_copy(step, peer, owner):
        rows = whole.at[rows_of(owner, share), :]
        return push(rows, rows, template_send.at[step], template_recv.at[step], "visit", peer)

    def patch_copy(source, target, send, recv, peer, sender):
        return push(source, target, send.at[peer], recv.at[sender], "patch", peer)

    def details_copy(peer, sender):
        return patch_copy(
            details_ref.at[peer], arrived_details.at[sender], details_send, details_recv, peer, sender
        )

    def tile_copy(peer, sender):
        return patch_copy(
            packed.at[rows_of(peer, tile_peer), :],
            arrived.at[rows_of(sender, tile_peer), :],
            tile_send,
            tile_recv,
            peer,
            sender,
        )

    def gram_copy(peer, sender):
        return patch_copy(gram.at[peer], grams.at[sender], gram_send, gram_recv, peer, sender)

    def solved_copy(peer, sender):
        return patch_copy(
            solved, arrived_solved.at[sender], solved_send, solved_recv, peer, sender
        )

    def model_copy(peer, sender):
        return patch_copy(
            model_packed.at[rows_of(peer, model_peer), :],
            returned.at[rows_of(sender, model_peer), :],
            model_send,
            model_recv,
            peer,
            sender,
        )

    def pack(peer):
        for n in range(capacity):
            slot = peer * capacity + n
            tile = local[slot // LANES, 5, slot % LANES]
            sigma = sigma_ref[tile] * local[slot // LANES, 6, slot % LANES].astype(jnp.float32)
            at = peer * tile_peer + n // group * tile_chunk + n % group * 4
            stage[pl.ds(at, 2), :] = science_ref[tile] * sigma
            stage[pl.ds(at + 2, 2), :] = sigma
        return stage[rows_of(peer, tile_peer), :].astype(jnp.bfloat16)

    barrier = pltpu.get_barrier_semaphore()
    peers_signal(barrier, "patch", me, patches)
    peers_signal(barrier, "visit", my_visit, visit_parts)
    bands = [
        pltpu.make_async_copy(row_band_in, row_band_ref, band_sem.at[0]),
        pltpu.make_async_copy(column_band_in, column_band_ref, band_sem.at[1]),
    ]
    for copy in bands:
        copy.start()
    whole[rows_of(my_visit, share), :] = template_ref[...].astype(jnp.bfloat16)
    pl.semaphore_wait(barrier, patches - 1 + visit_parts - 1)
    template_copy(0, far, my_visit).start()
    template_copy(1, near, my_visit).start()

    make_routes(patches, capacity, me, destination_ref, visit_ref, offsets_ref, details_ref, local_ref)
    own_scalars = pltpu.make_async_copy(local_ref, local, routes_sem.at[0])
    own_scalars.start()
    arrived_details[me] = details_ref[me]
    if tile_chunk != 4 * group:
        stage[...] = jnp.zeros_like(stage)
    running[slot_count] = jnp.zeros((ROWS, LANES), jnp.float32)
    filtered[:, :, patch_columns:] = jnp.zeros((NF, start_rows, LANES), jnp.bfloat16)
    template_copy(0, far, far).wait_recv()
    template_copy(2, near, far).start()
    own_scalars.wait()

    def pack_and_send(peer):
        details_copy(peer, me).start()
        packed[rows_of(peer, tile_peer), :] = pack(peer)
        tile_copy(peer, me).start()

    each_peer(pack_and_send)
    arrived[rows_of(me, tile_peer), :] = pack(me)
    template_copy(1, near, near).wait_recv()
    template_copy(2, near, lax.rem(near + 2, 4)).wait_recv()
    for copy in bands:
        copy.wait()

    for b in range(NF):
        filtered[b, :, :patch_columns] = jnp.dot(
            row_band_ref[b], whole[...], preferred_element_type=jnp.float32
        ).astype(jnp.bfloat16)

    def column_block(j, carry):
        at = pl.multiple_of(j * LANES, LANES)
        for b, first, indices in basis_runs():
            product = jnp.dot(
                filtered[b, :, pl.ds(at, 2 * LANES)],
                column_band_ref[:, first * LANES : (first + len(indices)) * LANES],
                preferred_element_type=jnp.float32,
            )
            for i, k in enumerate(indices):
                images[j, k * image_rows : k * image_rows + start_rows, :] = product[
                    :, i * LANES : (i + 1) * LANES
                ]
        return carry

    lax.fori_loop(0, patch_columns // LANES, column_block, 0)

    each_peer(lambda peer: details_copy(peer, peer).wait_recv())
    to_scalars = pltpu.make_async_copy(arrived_details, routes, routes_sem.at[1])
    to_scalars.start()
    to_scalars.wait()
    each_peer(lambda peer: tile_copy(peer, peer).wait_recv())

    lane = lax.broadcasted_iota(jnp.int32, (8, LANES), 1)
    eighth = lax.broadcasted_iota(jnp.int32, (8, LANES), 0)
    basis = lax.broadcasted_iota(jnp.int32, (ROWS, LANES), 0)
    part = lax.broadcasted_iota(jnp.int32, (ROWS, LANES), 1) // ROWS

    def pick(row, column):
        block = column // LANES
        shift = column % LANES
        halves = []
        for i in range(2):
            pieces = []
            for k in range(0, ROWS, 8):
                rows = pl.ds(k * image_rows + row + i, 8, stride=image_rows)
                piece = pltpu.roll(
                    jnp.where(lane >= shift, images[block, rows, :], images[block + 1, rows, :]),
                    (LANES - shift) % LANES,
                    axis=1,
                )
                if k + 8 >= NB:
                    constant = jnp.where(eighth + k == NB - 1, 1.0, 0.0)
                    piece = jnp.where(eighth + k < NB - 1, piece, constant)
                pieces.append(piece)
            halves.append(jnp.concatenate(pieces, axis=0))
        return halves

    def tile_group(g, carry):
        chunks = [
            arrived[rows_of(g * (GROUP // group) + c, tile_chunk), :].astype(jnp.float32)
            for c in range(GROUP // group)
        ]
        designs = []
        flags = []
        for t in range(GROUP):
            s = g * GROUP + t
            sender, n = s // capacity, s % capacity
            values = chunks[t // group][t % group * 4 : t % group * 4 + 4]
            halves = pick(routes[sender, 0, capacity + n], routes[sender, 0, 2 * capacity + n])
            flags.append(routes[sender, 0, 3 * capacity + n].astype(jnp.float32))
            for i in range(2):
                picked[s, i * ROWS : (i + 1) * ROWS, :] = halves[i]
            designs.append(
                jnp.concatenate(
                    [
                        jnp.where(
                            basis == RHS,
                            values[i : i + 1],
                            halves[i] * values[2 + i : 3 + i],
                        ).astype(jnp.bfloat16)
                        for i in range(2)
                    ],
                    axis=1,
                )
            )
        design = jnp.concatenate(designs, axis=0)
        products = lax.dot_general(
            design, design, (((1,), (1,)), ((), ())), preferred_element_type=jnp.float32
        )
        per = LANES // ROWS
        for t in range(GROUP):
            own = products[
                t * ROWS : (t + 1) * ROWS, (t // per) * LANES : (t // per + 1) * LANES
            ]
            carry = carry * flags[t] + jnp.where(part == t % per, own, 0.0)
            running[g * GROUP + t] = carry
        return carry

    def two_groups(h, carry):
        return tile_group(2 * h + 1, tile_group(2 * h, carry))

    lax.fori_loop(
        0, slot_count // GROUP // 2, two_groups, jnp.zeros((ROWS, LANES), jnp.float32)
    )

    lane_half = lax.broadcasted_iota(jnp.int32, (ROWS // 2, LANES), 1)
    diagonal = basis == lax.broadcasted_iota(jnp.int32, (ROWS, LANES), 1)

    def gram_of(owner):
        merged = jnp.zeros((ROWS, LANES), jnp.float32)
        for i in range(per_owner):
            v = owner * per_owner + i
            if patches <= VIS_DEV:
                folded = running[routes[0, 1, v]]
                for sender in range(1, patches):
                    folded = folded + running[routes[sender, 1, v]]
            else:
                folded = lax.fori_loop(
                    0,
                    patches,
                    lambda sender, sums: sums + running[routes[sender, 1, v]],
                    jnp.zeros((ROWS, LANES), jnp.float32),
                )
            folded = folded + pltpu.roll(folded, 2 * ROWS, axis=1)
            folded = folded + pltpu.roll(folded, ROWS, axis=1)
            merged = jnp.where(part == i, folded, merged)
        low = lane_half < LANES // 2
        return jnp.where(low, merged[: ROWS // 2], pltpu.roll(merged[ROWS // 2 :], LANES // 2, axis=1))

    def gram_and_send(peer):
        gram[peer] = gram_of(peer)
        gram_copy(peer, me).start()

    each_peer(lambda peer: when_owner(peer, lambda: gram_and_send(peer)))

    def solve_own():
        grams[me] = gram_of(me)
        each_peer(lambda peer: gram_copy(lax.rem(me, owners), peer).wait_recv())
        summed = jnp.sum(grams[...], axis=0)
        summed = jnp.concatenate([summed, pltpu.roll(summed, LANES // 2, axis=1)], axis=0)
        systems = [summed] + [
            pltpu.roll(summed, LANES - i * ROWS, axis=1) for i in range(1, per_owner)
        ]
        values = solve_systems(jnp.stack(systems, axis=0))
        merged = jnp.zeros((1, LANES), jnp.float32)
        for i in range(per_owner):
            as_row = jnp.sum(jnp.where(diagonal, values[i], 0.0), axis=0, keepdims=True)
            merged = merged + (pltpu.roll(as_row, i * ROWS, axis=1) if i else as_row)
        solved[...] = merged
        arrived_solved[me] = merged
        each_peer(lambda peer: solved_copy(peer, me).start())

    when_owner(me, solve_own)
    each_peer(lambda peer: when_owner(peer, lambda: solved_copy(peer, peer).wait_recv()))
    for v in range(VIS_DEV):
        i = v % per_owner
        as_row = arrived_solved[v // per_owner]
        as_row = pltpu.roll(as_row, LANES - i * ROWS, axis=1) if i else as_row
        coefficient_ref[v : v + 1, :] = as_row
        spread[v] = jnp.broadcast_to(
            jnp.sum(jnp.where(diagonal, as_row, 0.0), axis=1, keepdims=True), (ROWS, LANES)
        )

    def model_of(peer):
        for n in range(capacity):
            s = peer * capacity + n
            values = spread[routes[peer, 0, n]]
            at = peer * model_peer + n // group * model_chunk + n % group * 2
            for i in range(2):
                stage[pl.ds(at + i, 1), :] = jnp.sum(
                    picked[s, i * ROWS : (i + 1) * ROWS, :] * values, axis=0, keepdims=True
                )
        return stage[rows_of(peer, model_peer), :].astype(jnp.bfloat16)

    def model_and_send(peer):
        model_packed[rows_of(peer, model_peer), :] = model_of(peer)
        model_copy(peer, me).start()

    each_peer(model_and_send)
    returned[rows_of(me, model_peer), :] = model_of(me)
    template_copy(0, far, my_visit).wait_send()
    template_copy(1, near, my_visit).wait_send()
    template_copy(2, near, far).wait_send()

    def finish(peer):
        details_copy(peer, me).wait_send()
        tile_copy(peer, me).wait_send()
        when_owner(peer, lambda: gram_copy(peer, me).wait_send())
        when_owner(me, lambda: solved_copy(peer, me).wait_send())
        model_copy(peer, me).wait_send()
        model_copy(peer, peer).wait_recv()

    each_peer(finish)
    stage[: returned.shape[0], :] = returned[...].astype(jnp.float32)

    def give_back(q, carry):
        for t in range(2 * GROUP):
            tile = q * 2 * GROUP + t
            model_ref[tile] = stage[pl.ds(local[0, 7, tile], 2), :]
        return carry

    lax.fori_loop(0, model_ref.shape[0] // (2 * GROUP), give_back, 0)


def per_device(science, inverse_sigma, template, destination, offsets, visit_local):
    patches = lax.axis_size("patch")
    visit_parts = lax.axis_size("visit")
    tile_count, row_count, column_count = science.shape
    capacity = max(2, 2 * tile_count // patches)
    slot_count = patches * capacity
    patch_rows, patch_columns = template.shape[1] * visit_parts, template.shape[2]
    start_rows = -(-(patch_rows - 2 * KR) // 16) * 16
    image_rows = start_rows + 8
    row_band, column_band = band_tables(start_rows, patch_rows)
    group = min(GROUP, capacity)
    tile_total = slot_count // group * chunk_rows(group, 4)
    model_total = slot_count // group * chunk_rows(group, 2)

    owners = min(patches, VIS_DEV)
    vmem = pl.BlockSpec(memory_space=pltpu.VMEM)
    dma = pltpu.SemaphoreType.DMA
    wide, half = jnp.float32, jnp.bfloat16
    own_model, coefficients = pl.pallas_call(
        functools.partial(image_kernel, patches, visit_parts, capacity),
        out_shape=(
            jax.ShapeDtypeStruct(science.shape, wide),
            jax.ShapeDtypeStruct((VIS_DEV, LANES), wide),
        ),
        in_specs=[vmem] * 6 + [pl.BlockSpec(memory_space=pl.ANY)] * 2,
        out_specs=(vmem, vmem),
        scratch_shapes=[
            pltpu.VMEM((patch_rows, patch_columns), half),
            pltpu.VMEM((tile_total, LANES), half),
            pltpu.VMEM((patches, 2, LANES), jnp.int32),
            pltpu.SMEM((patches, 2, LANES), jnp.int32),
            pltpu.VMEM((patches, 2, LANES), jnp.int32),
            pltpu.VMEM((slot_count // LANES, 8, LANES), jnp.int32),
            pltpu.SMEM((slot_count // LANES, 8, LANES), jnp.int32),
            pltpu.VMEM(row_band.shape, half),
            pltpu.VMEM(column_band.shape, half),
            pltpu.VMEM((tile_total, LANES), wide),
            pltpu.VMEM((tile_total, LANES), half),
            pltpu.VMEM((NF, start_rows, patch_columns + LANES), half),
            pltpu.VMEM((patch_columns // LANES, image_rows * ROWS, LANES), wide),
            pltpu.VMEM((slot_count, row_count * ROWS, LANES), wide),
            pltpu.VMEM((slot_count + 1, ROWS, LANES), wide),
            pltpu.VMEM((owners, ROWS // 2, LANES), wide),
            pltpu.VMEM((patches, ROWS // 2, LANES), wide),
            pltpu.VMEM((1, LANES), wide),
            pltpu.VMEM((owners, 1, LANES), wide),
            pltpu.VMEM((VIS_DEV, ROWS, LANES), wide),
            pltpu.VMEM((model_total, LANES), half),
            pltpu.VMEM((model_total, LANES), half),
            dma((2,)),
            dma((2,)),
            dma((3,)),
            dma((3,)),
            dma((patches,)),
            dma((patches,)),
            dma((patches,)),
            dma((patches,)),
            dma((owners,)),
            dma((patches,)),
            dma((patches,)),
            dma((owners,)),
            dma((patches,)),
            dma((patches,)),
        ],
        compiler_params=pltpu.CompilerParams(
            vmem_limit_bytes=VMEM_BYTES, collective_id=0, has_side_effects=True
        ),
    )(
        destination.reshape(1, tile_count),
        visit_local.reshape(1, tile_count),
        offsets.T,
        template[0],
        science,
        inverse_sigma,
        row_band,
        column_band,
    )
    return (science - own_model, coefficients[:, :NB])


def solution(mesh):
    return jax.shard_map(
        per_device,
        mesh=mesh,
        in_specs=(
            P(("patch", "visit"), None, None),
            P(("patch", "visit"), None, None),
            P("patch", "visit", None),
            P(("patch", "visit")),
            P(("patch", "visit"), None),
            P(("patch", "visit")),
        ),
        out_specs=(P(("patch", "visit"), None, None), P("visit", None)),
        check_vma=False,
    )
```

```python
import functools

import jax
import jax.numpy as jnp
import numpy as np
from jax import lax
from jax.experimental import pallas as pl
from jax.experimental.pallas import tpu as pltpu
from jax.sharding import PartitionSpec as P

KR = 10
NF = 11
NB = 28
VIS_DEV = 16
ROWS = 32
RHS = 27
CONSTANT = 25
CLASSES = 8
GROUP = 8
LANES = 128
VMEM_BYTES = 60 * 1024 * 1024


gauss_widths = (1.0, 2.0, 4.0)
poly_degrees = (4, 2, 2)


def filter_table(radius):
    tap_points = np.arange(-radius, radius + 1) * 1.0
    raw_columns = []
    for width_value, degree in zip(gauss_widths, poly_degrees):
        bell_curve = np.exp(-tap_points * tap_points / (2.0 * width_value * width_value))
        for power_index in range(degree + 1):
            raw_columns.append(bell_curve * (tap_points / radius) ** power_index)
    orthonormal = []
    for column in raw_columns:
        vector = column.copy()
        for repeat_index in range(2):
            for earlier in orthonormal:
                vector = vector - np.dot(earlier, vector) * earlier
        orthonormal.append(vector / np.sqrt(np.dot(vector, vector)))
    return np.stack(orthonormal, axis=1).astype(np.float32)


def pair_layout():
    column_ids = []
    row_ids = []
    filter_runs = []
    offset = 0
    for degree in poly_degrees:
        for first_index in range(degree + 1):
            filter_runs.append((offset + first_index, offset, offset + degree - first_index + 1))
            for second_index in range(degree + 1 - first_index):
                column_ids.append(offset + first_index)
                row_ids.append(offset + second_index)
        offset += degree + 1
    return (column_ids, row_ids, filter_runs)


ENTRIES = (
    (0, 0, 0, 4, 0),
    (0, 1, 4, 1, 0),
    (1, 2, 0, 4, 0),
    (2, 3, 0, 3, 0),
    (3, 4, 0, 2, 0),
    (4, 1, 0, 1, 1),
    (5, 5, 5, 3, 0),
    (6, 4, 5, 2, 2),
    (7, 1, 5, 1, 2),
    (8, 6, 8, 3, 0),
    (9, 7, 8, 2, 0),
    (10, 7, 8, 1, 2),
)


def positions():
    column_ids, row_ids, _ = pair_layout()
    index_of = {pair: k for k, pair in enumerate(zip(column_ids, row_ids))}
    place = [CONSTANT] * NB
    for b, shift, first, count, group in ENTRIES:
        for i in range(count):
            place[index_of[(first + i, b)]] = (group + i) * CLASSES + shift
    return place


def band_tables(stored_rows, patch_rows):
    values = filter_table(KR)
    taps_count = 2 * KR + 1
    row_band = np.zeros((len(ENTRIES), stored_rows, patch_rows), np.float32)
    for e, (b, shift, _, _, _) in enumerate(ENTRIES):
        for start in range(patch_rows - taps_count + 1):
            row_band[e, start + shift, start : start + taps_count] = values[:, b]
    column_band = np.zeros((2 * LANES, NF, LANES), np.float32)
    for out_column in range(LANES):
        column_band[out_column : out_column + taps_count, :, out_column] = values
    return (
        jnp.asarray(row_band.astype(jnp.bfloat16)),
        jnp.asarray(column_band.reshape(2 * LANES, NF * LANES).astype(jnp.bfloat16)),
    )


def chunk_rows(group, per_tile):
    return -(-group * per_tile // 16) * 16


def peers_signal(barrier, axis, me, count):
    def one(i, carry):
        pl.semaphore_signal(
            barrier,
            inc=1,
            device_id={axis: lax.rem(me + 1 + i, count)},
            device_id_type=pl.DeviceIdType.MESH,
        )
        return carry

    lax.fori_loop(0, count - 1, one, 0)


def push(source, target, send_sem, recv_sem, axis, peer):
    return pltpu.make_async_remote_copy(
        src_ref=source,
        dst_ref=target,
        send_sem=send_sem,
        recv_sem=recv_sem,
        device_id={axis: peer},
        device_id_type=pl.DeviceIdType.MESH,
    )


def solve_systems(system):
    row_id = lax.broadcasted_iota(jnp.int32, system.shape, 1)
    column_id = lax.broadcasted_iota(jnp.int32, system.shape, 2)
    for p in positions():
        pivot_row = system[:, p : p + 1, :]
        inverse = 1.0 / system[:, p : p + 1, p : p + 1]
        factor = system[:, :, p : p + 1] * inverse
        system = jnp.where(row_id == p, system, system - factor * pivot_row)
    diagonal = jnp.sum(jnp.where(row_id == column_id, system, 0.0), axis=2, keepdims=True)
    solved = system[:, :, RHS : RHS + 1] / diagonal
    used = functools.reduce(jnp.logical_or, [row_id == p for p in positions()])
    return jnp.where(used, jnp.broadcast_to(solved, system.shape), 0.0)


def make_routes(
    patches, capacity, me, destination_ref, visit_ref, offsets_ref, details_ref, local_ref
):
    square = (LANES, LANES)
    lane = lax.broadcasted_iota(jnp.int32, square, 1)
    diagonal = lax.broadcasted_iota(jnp.int32, square, 0) == lane
    lane_row = lane[:1]
    slot_count = patches * capacity
    group = min(GROUP, capacity)
    chunk = chunk_rows(group, 2)

    def column(row):
        return jnp.sum(jnp.where(diagonal, row, 0), axis=1, keepdims=True)

    destination = destination_ref[...]
    key = (destination * VIS_DEV + visit_ref[...]) * LANES + lane_row
    key_column = column(key)
    pair_column = key_column // LANES
    patch_column = key_column // (LANES * VIS_DEV)
    earlier = (patch_column == destination) & (key_column < key)
    slot = destination * capacity + jnp.sum(jnp.where(earlier, 1, 0), axis=0, keepdims=True)
    slot_column = column(slot)
    rank_column = slot_column - patch_column * capacity
    values = [
        pair_column - patch_column * VIS_DEV,
        column(offsets_ref[0:1, :]),
        column(offsets_ref[1:2, :]),
        key_column - pair_column * LANES,
        jnp.ones((LANES, 1), jnp.int32),
    ]
    place = slot // group * chunk + slot % group * 2
    tables = []
    for block in range(slot_count // LANES):
        holds = slot_column == lane + block * LANES
        visit, row, col, order, live = [
            jnp.sum(jnp.where(holds, value, 0), axis=0, keepdims=True) for value in values
        ]
        follows = (visit == pltpu.roll(visit, 1, axis=1)) & (lane_row % capacity > 0) & (live > 0)
        tables.append([visit, row, col, jnp.where(follows, 1, 0)])
        local_ref[block] = jnp.concatenate(
            [visit, row, col, visit, visit, order, live, place], axis=0
        )
    for block in range(patches * VIS_DEV // LANES):
        found = jnp.max(
            jnp.where(pair_column == lane + block * LANES, rank_column, -1), axis=0, keepdims=True
        )
        last = jnp.where(
            found < 0, slot_count, jnp.minimum(found, capacity - 1) + me * capacity
        )
        for part in range(LANES // VIS_DEV):
            details_ref[block * (LANES // VIS_DEV) + part, 1:2, :] = (
                pltpu.roll(last, LANES - part * VIS_DEV, axis=1) if part else last
            )
    for patch in range(patches):
        table = tables[patch * capacity // LANES]
        merged = table[3]
        for q in range(4):
            shift = (q * capacity - patch * capacity) % LANES
            moved = pltpu.roll(table[q], shift, axis=1) if shift else table[q]
            merged = jnp.where(lane_row // capacity == q, moved, merged)
        details_ref[patch, 0:1, :] = merged


def image_kernel(
    patches,
    visit_parts,
    capacity,
    destination_ref,
    visit_ref,
    offsets_ref,
    template_ref,
    science_ref,
    sigma_ref,
    row_band_in,
    column_band_in,
    model_ref,
    coefficient_ref,
    whole,
    arrived,
    arrived_details,
    routes,
    details_ref,
    local_ref,
    local,
    row_band_ref,
    column_band_ref,
    stage,
    packed,
    filtered,
    images,
    picked,
    running,
    gram,
    grams,
    solved,
    arrived_solved,
    spread,
    model_packed,
    returned,
    routes_sem,
    band_sem,
    template_send,
    template_recv,
    tile_send,
    tile_recv,
    details_send,
    details_recv,
    gram_send,
    gram_recv,
    solved_send,
    solved_recv,
    model_send,
    model_recv,
):
    me = lax.axis_index("patch")
    my_visit = lax.axis_index("visit")
    slot_count = patches * capacity
    group = min(GROUP, capacity)
    tile_chunk = chunk_rows(group, 4)
    tile_peer = capacity // group * tile_chunk
    model_chunk = chunk_rows(group, 2)
    model_peer = capacity // group * model_chunk
    share, patch_columns = template_ref.shape
    stored_rows = row_band_ref.shape[1]
    image_rows = images.shape[1] // ROWS
    owners = gram.shape[0]
    per_owner = VIS_DEV // owners

    def rows_of(index, count):
        return pl.ds(pl.multiple_of(index * count, 16), count)

    def each_peer(action):
        def one(i, carry):
            action(lax.rem(me + 1 + i, patches))
            return carry

        lax.fori_loop(0, patches - 1, one, 0)

    def when_owner(index, action):
        if owners == patches:
            action()
        else:
            pl.when(index < owners)(action)

    near = my_visit + 1 - 2 * lax.rem(my_visit, 2)
    far = lax.rem(my_visit + 2, 4)

    def template_copy(step, peer, owner):
        rows = whole.at[rows_of(owner, share), :]
        return push(rows, rows, template_send.at[step], template_recv.at[step], "visit", peer)

    def patch_copy(source, target, send, recv, peer, sender):
        return push(source, target, send.at[peer], recv.at[sender], "patch", peer)

    def details_copy(peer, sender):
        return patch_copy(
            details_ref.at[peer], arrived_details.at[sender], details_send, details_recv, peer, sender
        )

    def tile_copy(peer, sender):
        return patch_copy(
            packed.at[rows_of(peer, tile_peer), :],
            arrived.at[rows_of(sender, tile_peer), :],
            tile_send,
            tile_recv,
            peer,
            sender,
        )

    def gram_copy(peer, sender):
        return patch_copy(gram.at[peer], grams.at[sender], gram_send, gram_recv, peer, sender)

    def solved_copy(peer, sender):
        return patch_copy(
            solved, arrived_solved.at[sender], solved_send, solved_recv, peer, sender
        )

    def model_copy(peer, sender):
        return patch_copy(
            model_packed.at[rows_of(peer, model_peer), :],
            returned.at[rows_of(sender, model_peer), :],
            model_send,
            model_recv,
            peer,
            sender,
        )

    def pack(peer):
        for n in range(capacity):
            slot = peer * capacity + n
            tile = local[slot // LANES, 5, slot % LANES]
            sigma = sigma_ref[tile] * local[slot // LANES, 6, slot % LANES].astype(jnp.float32)
            at = peer * tile_peer + n // group * tile_chunk + n % group * 4
            stage[pl.ds(at, 2), :] = science_ref[tile] * sigma
            stage[pl.ds(at + 2, 2), :] = sigma
        return stage[rows_of(peer, tile_peer), :].astype(jnp.bfloat16)

    barrier = pltpu.get_barrier_semaphore()
    peers_signal(barrier, "patch", me, patches)
    peers_signal(barrier, "visit", my_visit, visit_parts)
    bands = [
        pltpu.make_async_copy(row_band_in, row_band_ref, band_sem.at[0]),
        pltpu.make_async_copy(column_band_in, column_band_ref, band_sem.at[1]),
    ]
    for copy in bands:
        copy.start()
    whole[rows_of(my_visit, share), :] = template_ref[...].astype(jnp.bfloat16)
    pl.semaphore_wait(barrier, patches - 1 + visit_parts - 1)
    template_copy(0, far, my_visit).start()
    template_copy(1, near, my_visit).start()

    make_routes(patches, capacity, me, destination_ref, visit_ref, offsets_ref, details_ref, local_ref)
    own_scalars = pltpu.make_async_copy(local_ref, local, routes_sem.at[0])
    own_scalars.start()
    arrived_details[me] = details_ref[me]
    if tile_chunk != 4 * group:
        stage[...] = jnp.zeros_like(stage)
    running[slot_count] = jnp.zeros((ROWS, LANES), jnp.float32)
    filtered[:, :, patch_columns:] = jnp.zeros((len(ENTRIES), stored_rows, LANES), jnp.bfloat16)
    template_copy(0, far, far).wait_recv()
    template_copy(2, near, far).start()
    own_scalars.wait()

    def pack_and_send(peer):
        details_copy(peer, me).start()
        packed[rows_of(peer, tile_peer), :] = pack(peer)
        tile_copy(peer, me).start()

    each_peer(pack_and_send)
    arrived[rows_of(me, tile_peer), :] = pack(me)
    template_copy(1, near, near).wait_recv()
    template_copy(2, near, lax.rem(near + 2, 4)).wait_recv()
    for copy in bands:
        copy.wait()

    for e in range(len(ENTRIES)):
        filtered[e, :, :patch_columns] = jnp.dot(
            row_band_ref[e], whole[...], preferred_element_type=jnp.float32
        ).astype(jnp.bfloat16)

    def column_block(j, carry):
        at = pl.multiple_of(j * LANES, LANES)
        for e, (_, shift, first, count, group_at) in enumerate(ENTRIES):
            product = jnp.dot(
                filtered[e, :, pl.ds(at, 2 * LANES)],
                column_band_ref[:, first * LANES : (first + count) * LANES],
                preferred_element_type=jnp.float32,
            )
            for i in range(count):
                base = ((group_at + i) * CLASSES + shift) * image_rows
                images[j, base : base + image_rows, :] = product[
                    :image_rows, i * LANES : (i + 1) * LANES
                ]
        return carry

    lax.fori_loop(0, patch_columns // LANES, column_block, 0)

    each_peer(lambda peer: details_copy(peer, peer).wait_recv())
    to_scalars = pltpu.make_async_copy(arrived_details, routes, routes_sem.at[1])
    to_scalars.start()
    to_scalars.wait()
    each_peer(lambda peer: tile_copy(peer, peer).wait_recv())

    lane = lax.broadcasted_iota(jnp.int32, (8, LANES), 1)
    eighth = lax.broadcasted_iota(jnp.int32, (8, LANES), 0)
    basis = lax.broadcasted_iota(jnp.int32, (ROWS, LANES), 0)
    part = lax.broadcasted_iota(jnp.int32, (ROWS, LANES), 1) // ROWS

    def pick(row, column):
        block = column // LANES
        shift = column % LANES
        halves = []
        for i in range(2):
            pieces = []
            for k in range(0, ROWS, 8):
                rows = pl.ds(k * image_rows + row + i, CLASSES, stride=image_rows + 1)
                piece = pltpu.roll(
                    jnp.where(lane >= shift, images[block, rows, :], images[block + 1, rows, :]),
                    (LANES - shift) % LANES,
                    axis=1,
                )
                if k + CLASSES == ROWS:
                    kept = functools.reduce(
                        jnp.logical_or, [eighth + k == p for p in positions()[:-1] if p >= k]
                    )
                    piece = jnp.where(kept, piece, jnp.where(eighth + k == CONSTANT, 1.0, 0.0))
                pieces.append(piece)
            halves.append(jnp.concatenate(pieces, axis=0))
        return halves

    def tile_group(g, carry):
        chunks = [
            arrived[rows_of(g * (GROUP // group) + c, tile_chunk), :].astype(jnp.float32)
            for c in range(GROUP // group)
        ]
        designs = []
        flags = []
        for t in range(GROUP):
            s = g * GROUP + t
            sender, n = s // capacity, s % capacity
            values = chunks[t // group][t % group * 4 : t % group * 4 + 4]
            halves = pick(routes[sender, 0, capacity + n], routes[sender, 0, 2 * capacity + n])
            flags.append(routes[sender, 0, 3 * capacity + n].astype(jnp.float32))
            for i in range(2):
                picked[s, i * ROWS : (i + 1) * ROWS, :] = halves[i]
            designs.append(
                jnp.concatenate(
                    [
                        jnp.where(
                            basis == RHS,
                            values[i : i + 1],
                            halves[i] * values[2 + i : 3 + i],
                        ).astype(jnp.bfloat16)
                        for i in range(2)
                    ],
                    axis=1,
                )
            )
        design = jnp.concatenate(designs, axis=0)
        products = lax.dot_general(
            design, design, (((1,), (1,)), ((), ())), preferred_element_type=jnp.float32
        )
        per = LANES // ROWS
        for t in range(GROUP):
            own = products[
                t * ROWS : (t + 1) * ROWS, (t // per) * LANES : (t // per + 1) * LANES
            ]
            carry = carry * flags[t] + jnp.where(part == t % per, own, 0.0)
            running[g * GROUP + t] = carry
        return carry

    def two_groups(h, carry):
        return tile_group(2 * h + 1, tile_group(2 * h, carry))

    lax.fori_loop(
        0, slot_count // GROUP // 2, two_groups, jnp.zeros((ROWS, LANES), jnp.float32)
    )

    lane_half = lax.broadcasted_iota(jnp.int32, (ROWS // 2, LANES), 1)
    basis_lane = lax.broadcasted_iota(jnp.int32, (ROWS, LANES), 1)
    diagonal = functools.reduce(
        jnp.logical_or, [(basis == p) & (basis_lane == k) for k, p in enumerate(positions())]
    )

    def gram_of(owner):
        merged = jnp.zeros((ROWS, LANES), jnp.float32)
        for i in range(per_owner):
            v = owner * per_owner + i
            if patches <= VIS_DEV:
                folded = running[routes[0, 1, v]]
                for sender in range(1, patches):
                    folded = folded + running[routes[sender, 1, v]]
            else:
                folded = lax.fori_loop(
                    0,
                    patches,
                    lambda sender, sums: sums + running[routes[sender, 1, v]],
                    jnp.zeros((ROWS, LANES), jnp.float32),
                )
            folded = folded + pltpu.roll(folded, 2 * ROWS, axis=1)
            folded = folded + pltpu.roll(folded, ROWS, axis=1)
            merged = jnp.where(part == i, folded, merged)
        low = lane_half < LANES // 2
        return jnp.where(low, merged[: ROWS // 2], pltpu.roll(merged[ROWS // 2 :], LANES // 2, axis=1))

    def gram_and_send(peer):
        gram[peer] = gram_of(peer)
        gram_copy(peer, me).start()

    each_peer(lambda peer: when_owner(peer, lambda: gram_and_send(peer)))

    def solve_own():
        grams[me] = gram_of(me)
        each_peer(lambda peer: gram_copy(lax.rem(me, owners), peer).wait_recv())
        summed = jnp.sum(grams[...], axis=0)
        summed = jnp.concatenate([summed, pltpu.roll(summed, LANES // 2, axis=1)], axis=0)
        systems = [summed] + [
            pltpu.roll(summed, LANES - i * ROWS, axis=1) for i in range(1, per_owner)
        ]
        values = solve_systems(jnp.stack(systems, axis=0))
        merged = jnp.zeros((1, LANES), jnp.float32)
        for i in range(per_owner):
            as_row = jnp.sum(jnp.where(diagonal, values[i], 0.0), axis=0, keepdims=True)
            merged = merged + (pltpu.roll(as_row, i * ROWS, axis=1) if i else as_row)
        solved[...] = merged
        arrived_solved[me] = merged
        each_peer(lambda peer: solved_copy(peer, me).start())

    when_owner(me, solve_own)
    each_peer(lambda peer: when_owner(peer, lambda: solved_copy(peer, peer).wait_recv()))
    for v in range(VIS_DEV):
        i = v % per_owner
        as_row = arrived_solved[v // per_owner]
        as_row = pltpu.roll(as_row, LANES - i * ROWS, axis=1) if i else as_row
        coefficient_ref[v : v + 1, :] = as_row
        spread[v] = jnp.broadcast_to(
            jnp.sum(jnp.where(diagonal, as_row, 0.0), axis=1, keepdims=True), (ROWS, LANES)
        )

    def model_of(peer):
        for n in range(capacity):
            s = peer * capacity + n
            values = spread[routes[peer, 0, n]]
            at = peer * model_peer + n // group * model_chunk + n % group * 2
            for i in range(2):
                stage[pl.ds(at + i, 1), :] = jnp.sum(
                    picked[s, i * ROWS : (i + 1) * ROWS, :] * values, axis=0, keepdims=True
                )
        return stage[rows_of(peer, model_peer), :].astype(jnp.bfloat16)

    def model_and_send(peer):
        model_packed[rows_of(peer, model_peer), :] = model_of(peer)
        model_copy(peer, me).start()

    each_peer(model_and_send)
    returned[rows_of(me, model_peer), :] = model_of(me)
    template_copy(0, far, my_visit).wait_send()
    template_copy(1, near, my_visit).wait_send()
    template_copy(2, near, far).wait_send()

    def finish(peer):
        details_copy(peer, me).wait_send()
        tile_copy(peer, me).wait_send()
        when_owner(peer, lambda: gram_copy(peer, me).wait_send())
        when_owner(me, lambda: solved_copy(peer, me).wait_send())
        model_copy(peer, me).wait_send()
        model_copy(peer, peer).wait_recv()

    each_peer(finish)
    stage[: returned.shape[0], :] = returned[...].astype(jnp.float32)

    def give_back(q, carry):
        for t in range(2 * GROUP):
            tile = q * 2 * GROUP + t
            model_ref[tile] = stage[pl.ds(local[0, 7, tile], 2), :]
        return carry

    lax.fori_loop(0, model_ref.shape[0] // (2 * GROUP), give_back, 0)


def per_device(science, inverse_sigma, template, destination, offsets, visit_local):
    patches = lax.axis_size("patch")
    visit_parts = lax.axis_size("visit")
    tile_count, row_count, column_count = science.shape
    capacity = max(2, 2 * tile_count // patches)
    slot_count = patches * capacity
    patch_rows, patch_columns = template.shape[1] * visit_parts, template.shape[2]
    image_rows = -(-(patch_rows - 2 * KR + CLASSES - 1) // 8) * 8
    stored_rows = -(-image_rows // 16) * 16
    row_band, column_band = band_tables(stored_rows, patch_rows)
    group = min(GROUP, capacity)
    tile_total = slot_count // group * chunk_rows(group, 4)
    model_total = slot_count // group * chunk_rows(group, 2)

    owners = min(patches, VIS_DEV)
    vmem = pl.BlockSpec(memory_space=pltpu.VMEM)
    dma = pltpu.SemaphoreType.DMA
    wide, half = jnp.float32, jnp.bfloat16
    own_model, coefficients = pl.pallas_call(
        functools.partial(image_kernel, patches, visit_parts, capacity),
        out_shape=(
            jax.ShapeDtypeStruct(science.shape, wide),
            jax.ShapeDtypeStruct((VIS_DEV, LANES), wide),
        ),
        in_specs=[vmem] * 6 + [pl.BlockSpec(memory_space=pl.ANY)] * 2,
        out_specs=(vmem, vmem),
        scratch_shapes=[
            pltpu.VMEM((patch_rows, patch_columns), half),
            pltpu.VMEM((tile_total, LANES), half),
            pltpu.VMEM((patches, 2, LANES), jnp.int32),
            pltpu.SMEM((patches, 2, LANES), jnp.int32),
            pltpu.VMEM((patches, 2, LANES), jnp.int32),
            pltpu.VMEM((slot_count // LANES, 8, LANES), jnp.int32),
            pltpu.SMEM((slot_count // LANES, 8, LANES), jnp.int32),
            pltpu.VMEM(row_band.shape, half),
            pltpu.VMEM(column_band.shape, half),
            pltpu.VMEM((tile_total, LANES), wide),
            pltpu.VMEM((tile_total, LANES), half),
            pltpu.VMEM((len(ENTRIES), stored_rows, patch_columns + LANES), half),
            pltpu.VMEM((patch_columns // LANES, image_rows * ROWS, LANES), wide),
            pltpu.VMEM((slot_count, row_count * ROWS, LANES), wide),
            pltpu.VMEM((slot_count + 1, ROWS, LANES), wide),
            pltpu.VMEM((owners, ROWS // 2, LANES), wide),
            pltpu.VMEM((patches, ROWS // 2, LANES), wide),
            pltpu.VMEM((1, LANES), wide),
            pltpu.VMEM((owners, 1, LANES), wide),
            pltpu.VMEM((VIS_DEV, ROWS, LANES), wide),
            pltpu.VMEM((model_total, LANES), half),
            pltpu.VMEM((model_total, LANES), half),
            dma((2,)),
            dma((2,)),
            dma((3,)),
            dma((3,)),
            dma((patches,)),
            dma((patches,)),
            dma((patches,)),
            dma((patches,)),
            dma((owners,)),
            dma((patches,)),
            dma((patches,)),
            dma((owners,)),
            dma((patches,)),
            dma((patches,)),
        ],
        compiler_params=pltpu.CompilerParams(
            vmem_limit_bytes=VMEM_BYTES, collective_id=0, has_side_effects=True
        ),
    )(
        destination.reshape(1, tile_count),
        visit_local.reshape(1, tile_count),
        offsets.T,
        template[0],
        science,
        inverse_sigma,
        row_band,
        column_band,
    )
    return (science - own_model, coefficients[:, :NB])


def solution(mesh):
    return jax.shard_map(
        per_device,
        mesh=mesh,
        in_specs=(
            P(("patch", "visit"), None, None),
            P(("patch", "visit"), None, None),
            P("patch", "visit", None),
            P(("patch", "visit")),
            P(("patch", "visit"), None),
            P(("patch", "visit")),
        ),
        out_specs=(P(("patch", "visit"), None, None), P("visit", None)),
        check_vma=False,
    )
```

```python
import functools

import jax
import jax.numpy as jnp
import numpy as np
from jax import lax
from jax.experimental import pallas as pl
from jax.experimental.pallas import tpu as pltpu
from jax.sharding import PartitionSpec as P

KR = 10
NF = 11
NB = 28
VIS_DEV = 16
ROWS = 32
RHS = NB
GROUP = 8
LANES = 128
VMEM_BYTES = 60 * 1024 * 1024


gauss_widths = (1.0, 2.0, 4.0)
poly_degrees = (4, 2, 2)


def filter_table(radius):
    tap_points = np.arange(-radius, radius + 1) * 1.0
    raw_columns = []
    for width_value, degree in zip(gauss_widths, poly_degrees):
        bell_curve = np.exp(-tap_points * tap_points / (2.0 * width_value * width_value))
        for power_index in range(degree + 1):
            raw_columns.append(bell_curve * (tap_points / radius) ** power_index)
    orthonormal = []
    for column in raw_columns:
        vector = column.copy()
        for repeat_index in range(2):
            for earlier in orthonormal:
                vector = vector - np.dot(earlier, vector) * earlier
        orthonormal.append(vector / np.sqrt(np.dot(vector, vector)))
    return np.stack(orthonormal, axis=1).astype(np.float32)


def pair_layout():
    column_ids = []
    row_ids = []
    filter_runs = []
    offset = 0
    for degree in poly_degrees:
        for first_index in range(degree + 1):
            filter_runs.append((offset + first_index, offset, offset + degree - first_index + 1))
            for second_index in range(degree + 1 - first_index):
                column_ids.append(offset + first_index)
                row_ids.append(offset + second_index)
        offset += degree + 1
    return (column_ids, row_ids, filter_runs)


def band_tables(start_rows, patch_rows):
    values = filter_table(KR)
    taps_count = 2 * KR + 1
    row_band = np.zeros((NF, start_rows, patch_rows), np.float32)
    for start in range(start_rows):
        stop = min(start + taps_count, patch_rows)
        row_band[:, start, start:stop] = values.T[:, : stop - start]
    column_band = np.zeros((2 * LANES, NF, LANES), np.float32)
    for out_column in range(LANES):
        column_band[out_column : out_column + taps_count, :, out_column] = values
    return (
        jnp.asarray(row_band.astype(jnp.bfloat16)),
        jnp.asarray(column_band.reshape(2 * LANES, NF * LANES).astype(jnp.bfloat16)),
    )


def basis_runs():
    column_ids, row_ids, _ = pair_layout()
    index_of = {pair: k for k, pair in enumerate(zip(column_ids, row_ids))}
    runs = []
    offset = 0
    for degree in poly_degrees:
        for second in range(degree + 1):
            b = offset + second
            count = degree + 1 - second
            runs.append((b, offset, [index_of[(offset + i, b)] for i in range(count)]))
        offset += degree + 1
    return runs


def chunk_rows(group, per_tile):
    return -(-group * per_tile // 16) * 16


def peers_signal(barrier, axis, me, count):
    def one(i, carry):
        pl.semaphore_signal(
            barrier,
            inc=1,
            device_id={axis: lax.rem(me + 1 + i, count)},
            device_id_type=pl.DeviceIdType.MESH,
        )
        return carry

    lax.fori_loop(0, count - 1, one, 0)


def push(source, target, send_sem, recv_sem, axis, peer):
    return pltpu.make_async_remote_copy(
        src_ref=source,
        dst_ref=target,
        send_sem=send_sem,
        recv_sem=recv_sem,
        device_id={axis: peer},
        device_id_type=pl.DeviceIdType.MESH,
    )


def solve_systems(system):
    row_id = lax.broadcasted_iota(jnp.int32, system.shape, 1)
    for p in range(0, NB, 2):
        q = p + 1
        top, low = system[:, p : p + 1, :], system[:, q : q + 1, :]
        a, b = system[:, p : p + 1, p : p + 1], system[:, p : p + 1, q : q + 1]
        c, d = system[:, q : q + 1, p : p + 1], system[:, q : q + 1, q : q + 1]
        ratio = c / a
        schur = 1.0 / (d - ratio * b)
        low = (low - ratio * top) * schur
        top = (top - b * low) / a
        left, right = system[:, :, p : p + 1], system[:, :, q : q + 1]
        reduced = system - left * top - right * low
        system = jnp.where(row_id == p, top, jnp.where(row_id == q, low, reduced))
    solved = system[:, :, RHS : RHS + 1]
    return jnp.where(row_id < NB, jnp.broadcast_to(solved, system.shape), 0.0)


def make_routes(
    patches, capacity, me, destination_ref, visit_ref, offsets_ref, details_ref, local_ref
):
    square = (LANES, LANES)
    lane = lax.broadcasted_iota(jnp.int32, square, 1)
    diagonal = lax.broadcasted_iota(jnp.int32, square, 0) == lane
    lane_row = lane[:1]
    slot_count = patches * capacity
    group = min(GROUP, capacity)
    chunk = chunk_rows(group, 2)

    def column(row):
        return jnp.sum(jnp.where(diagonal, row, 0), axis=1, keepdims=True)

    destination = destination_ref[...]
    key = (destination * VIS_DEV + visit_ref[...]) * LANES + lane_row
    key_column = column(key)
    pair_column = key_column // LANES
    patch_column = key_column // (LANES * VIS_DEV)
    earlier = (patch_column == destination) & (key_column < key)
    slot = destination * capacity + jnp.sum(jnp.where(earlier, 1, 0), axis=0, keepdims=True)
    slot_column = column(slot)
    rank_column = slot_column - patch_column * capacity
    values = [
        pair_column - patch_column * VIS_DEV,
        column(offsets_ref[0:1, :]),
        column(offsets_ref[1:2, :]),
        key_column - pair_column * LANES,
        jnp.ones((LANES, 1), jnp.int32),
    ]
    place = slot // group * chunk + slot % group * 2
    tables = []
    for block in range(slot_count // LANES):
        holds = slot_column == lane + block * LANES
        visit, row, col, order, live = [
            jnp.sum(jnp.where(holds, value, 0), axis=0, keepdims=True) for value in values
        ]
        follows = (visit == pltpu.roll(visit, 1, axis=1)) & (lane_row % capacity > 0) & (live > 0)
        tables.append([visit, row, col, jnp.where(follows, 1, 0)])
        local_ref[block] = jnp.concatenate(
            [visit, row, col, visit, visit, order, live, place], axis=0
        )
    for block in range(patches * VIS_DEV // LANES):
        found = jnp.max(
            jnp.where(pair_column == lane + block * LANES, rank_column, -1), axis=0, keepdims=True
        )
        last = jnp.where(
            found < 0, slot_count, jnp.minimum(found, capacity - 1) + me * capacity
        )
        for part in range(LANES // VIS_DEV):
            details_ref[block * (LANES // VIS_DEV) + part, 1:2, :] = (
                pltpu.roll(last, LANES - part * VIS_DEV, axis=1) if part else last
            )
    for patch in range(patches):
        table = tables[patch * capacity // LANES]
        merged = table[3]
        for q in range(4):
            shift = (q * capacity - patch * capacity) % LANES
            moved = pltpu.roll(table[q], shift, axis=1) if shift else table[q]
            merged = jnp.where(lane_row // capacity == q, moved, merged)
        details_ref[patch, 0:1, :] = merged


def image_kernel(
    patches,
    visit_parts,
    capacity,
    destination_ref,
    visit_ref,
    offsets_ref,
    template_ref,
    science_ref,
    sigma_ref,
    row_band_in,
    column_band_in,
    model_ref,
    coefficient_ref,
    whole,
    arrived,
    arrived_details,
    routes,
    details_ref,
    local_ref,
    local,
    row_band_ref,
    column_band_ref,
    stage,
    packed,
    filtered,
    images,
    picked,
    running,
    gram,
    grams,
    solved,
    arrived_solved,
    spread,
    model_packed,
    returned,
    routes_sem,
    band_sem,
    template_send,
    template_recv,
    tile_send,
    tile_recv,
    details_send,
    details_recv,
    gram_send,
    gram_recv,
    solved_send,
    solved_recv,
    model_send,
    model_recv,
):
    me = lax.axis_index("patch")
    my_visit = lax.axis_index("visit")
    slot_count = patches * capacity
    group = min(GROUP, capacity)
    tile_chunk = chunk_rows(group, 4)
    tile_peer = capacity // group * tile_chunk
    model_chunk = chunk_rows(group, 2)
    model_peer = capacity // group * model_chunk
    share, patch_columns = template_ref.shape
    start_rows = row_band_ref.shape[1]
    image_rows = images.shape[1] // ROWS
    owners = gram.shape[0]
    per_owner = VIS_DEV // owners

    def rows_of(index, count):
        return pl.ds(pl.multiple_of(index * count, 16), count)

    def each_peer(action):
        def one(i, carry):
            action(lax.rem(me + 1 + i, patches))
            return carry

        lax.fori_loop(0, patches - 1, one, 0)

    def when_owner(index, action):
        if owners == patches:
            action()
        else:
            pl.when(index < owners)(action)

    near = my_visit + 1 - 2 * lax.rem(my_visit, 2)
    far = lax.rem(my_visit + 2, 4)

    def template_copy(step, peer, owner):
        rows = whole.at[rows_of(owner, share), :]
        return push(rows, rows, template_send.at[step], template_recv.at[step], "visit", peer)

    def patch_copy(source, target, send, recv, peer, sender):
        return push(source, target, send.at[peer], recv.at[sender], "patch", peer)

    def details_copy(peer, sender):
        return patch_copy(
            details_ref.at[peer], arrived_details.at[sender], details_send, details_recv, peer, sender
        )

    def tile_copy(peer, sender):
        return patch_copy(
            packed.at[rows_of(peer, tile_peer), :],
            arrived.at[rows_of(sender, tile_peer), :],
            tile_send,
            tile_recv,
            peer,
            sender,
        )

    def gram_copy(peer, sender):
        return patch_copy(gram.at[peer], grams.at[sender], gram_send, gram_recv, peer, sender)

    def solved_copy(peer, sender):
        return patch_copy(
            solved, arrived_solved.at[sender], solved_send, solved_recv, peer, sender
        )

    def model_copy(peer, sender):
        return patch_copy(
            model_packed.at[rows_of(peer, model_peer), :],
            returned.at[rows_of(sender, model_peer), :],
            model_send,
            model_recv,
            peer,
            sender,
        )

    def pack(peer):
        for n in range(capacity):
            slot = peer * capacity + n
            tile = local[slot // LANES, 5, slot % LANES]
            sigma = sigma_ref[tile] * local[slot // LANES, 6, slot % LANES].astype(jnp.float32)
            at = peer * tile_peer + n // group * tile_chunk + n % group * 4
            stage[pl.ds(at, 2), :] = science_ref[tile] * sigma
            stage[pl.ds(at + 2, 2), :] = sigma
        return stage[rows_of(peer, tile_peer), :].astype(jnp.bfloat16)

    barrier = pltpu.get_barrier_semaphore()
    peers_signal(barrier, "patch", me, patches)
    peers_signal(barrier, "visit", my_visit, visit_parts)
    bands = [
        pltpu.make_async_copy(row_band_in, row_band_ref, band_sem.at[0]),
        pltpu.make_async_copy(column_band_in, column_band_ref, band_sem.at[1]),
    ]
    for copy in bands:
        copy.start()
    whole[rows_of(my_visit, share), :] = template_ref[...].astype(jnp.bfloat16)
    pl.semaphore_wait(barrier, patches - 1 + visit_parts - 1)
    template_copy(0, far, my_visit).start()
    template_copy(1, near, my_visit).start()

    make_routes(patches, capacity, me, destination_ref, visit_ref, offsets_ref, details_ref, local_ref)
    own_scalars = pltpu.make_async_copy(local_ref, local, routes_sem.at[0])
    own_scalars.start()
    arrived_details[me] = details_ref[me]
    if tile_chunk != 4 * group:
        stage[...] = jnp.zeros_like(stage)
    running[slot_count] = jnp.zeros((ROWS, LANES), jnp.float32)
    filtered[:, :, patch_columns:] = jnp.zeros((NF, start_rows, LANES), jnp.bfloat16)
    template_copy(0, far, far).wait_recv()
    template_copy(2, near, far).start()
    own_scalars.wait()

    def pack_and_send(peer):
        details_copy(peer, me).start()
        packed[rows_of(peer, tile_peer), :] = pack(peer)
        tile_copy(peer, me).start()

    each_peer(pack_and_send)
    arrived[rows_of(me, tile_peer), :] = pack(me)
    template_copy(1, near, near).wait_recv()
    template_copy(2, near, lax.rem(near + 2, 4)).wait_recv()
    for copy in bands:
        copy.wait()

    for b in range(NF):
        filtered[b, :, :patch_columns] = jnp.dot(
            row_band_ref[b], whole[...], preferred_element_type=jnp.float32
        ).astype(jnp.bfloat16)

    def column_block(j, carry):
        at = pl.multiple_of(j * LANES, LANES)
        for b, first, indices in basis_runs():
            product = jnp.dot(
                filtered[b, :, pl.ds(at, 2 * LANES)],
                column_band_ref[:, first * LANES : (first + len(indices)) * LANES],
                preferred_element_type=jnp.float32,
            )
            for i, k in enumerate(indices):
                images[j, k * image_rows : k * image_rows + start_rows, :] = product[
                    :, i * LANES : (i + 1) * LANES
                ]
        return carry

    lax.fori_loop(0, patch_columns // LANES, column_block, 0)

    each_peer(lambda peer: details_copy(peer, peer).wait_recv())
    to_scalars = pltpu.make_async_copy(arrived_details, routes, routes_sem.at[1])
    to_scalars.start()
    to_scalars.wait()
    each_peer(lambda peer: tile_copy(peer, peer).wait_recv())

    lane = lax.broadcasted_iota(jnp.int32, (8, LANES), 1)
    eighth = lax.broadcasted_iota(jnp.int32, (8, LANES), 0)
    basis = lax.broadcasted_iota(jnp.int32, (ROWS, LANES), 0)
    part = lax.broadcasted_iota(jnp.int32, (ROWS, LANES), 1) // ROWS

    def pick(row, column):
        block = column // LANES
        shift = column % LANES
        halves = []
        for i in range(2):
            pieces = []
            for k in range(0, ROWS, 8):
                rows = pl.ds(k * image_rows + row + i, 8, stride=image_rows)
                piece = pltpu.roll(
                    jnp.where(lane >= shift, images[block, rows, :], images[block + 1, rows, :]),
                    (LANES - shift) % LANES,
                    axis=1,
                )
                if k + 8 >= NB:
                    constant = jnp.where(eighth + k == NB - 1, 1.0, 0.0)
                    piece = jnp.where(eighth + k < NB - 1, piece, constant)
                pieces.append(piece)
            halves.append(jnp.concatenate(pieces, axis=0))
        return halves

    def tile_group(g, carry):
        chunks = [
            arrived[rows_of(g * (GROUP // group) + c, tile_chunk), :].astype(jnp.float32)
            for c in range(GROUP // group)
        ]
        designs = []
        flags = []
        for t in range(GROUP):
            s = g * GROUP + t
            sender, n = s // capacity, s % capacity
            values = chunks[t // group][t % group * 4 : t % group * 4 + 4]
            halves = pick(routes[sender, 0, capacity + n], routes[sender, 0, 2 * capacity + n])
            flags.append(routes[sender, 0, 3 * capacity + n].astype(jnp.float32))
            for i in range(2):
                picked[s, i * ROWS : (i + 1) * ROWS, :] = halves[i]
            designs.append(
                jnp.concatenate(
                    [
                        jnp.where(
                            basis == RHS,
                            values[i : i + 1],
                            halves[i] * values[2 + i : 3 + i],
                        ).astype(jnp.bfloat16)
                        for i in range(2)
                    ],
                    axis=1,
                )
            )
        design = jnp.concatenate(designs, axis=0)
        products = lax.dot_general(
            design, design, (((1,), (1,)), ((), ())), preferred_element_type=jnp.float32
        )
        per = LANES // ROWS
        for t in range(GROUP):
            own = products[
                t * ROWS : (t + 1) * ROWS, (t // per) * LANES : (t // per + 1) * LANES
            ]
            carry = carry * flags[t] + jnp.where(part == t % per, own, 0.0)
            running[g * GROUP + t] = carry
        return carry

    def two_groups(h, carry):
        return tile_group(2 * h + 1, tile_group(2 * h, carry))

    lax.fori_loop(
        0, slot_count // GROUP // 2, two_groups, jnp.zeros((ROWS, LANES), jnp.float32)
    )

    lane_half = lax.broadcasted_iota(jnp.int32, (ROWS // 2, LANES), 1)
    diagonal = basis == lax.broadcasted_iota(jnp.int32, (ROWS, LANES), 1)

    def gram_of(owner):
        merged = jnp.zeros((ROWS, LANES), jnp.float32)
        for i in range(per_owner):
            v = owner * per_owner + i
            if patches <= VIS_DEV:
                folded = running[routes[0, 1, v]]
                for sender in range(1, patches):
                    folded = folded + running[routes[sender, 1, v]]
            else:
                folded = lax.fori_loop(
                    0,
                    patches,
                    lambda sender, sums: sums + running[routes[sender, 1, v]],
                    jnp.zeros((ROWS, LANES), jnp.float32),
                )
            folded = folded + pltpu.roll(folded, 2 * ROWS, axis=1)
            folded = folded + pltpu.roll(folded, ROWS, axis=1)
            merged = jnp.where(part == i, folded, merged)
        low = lane_half < LANES // 2
        return jnp.where(low, merged[: ROWS // 2], pltpu.roll(merged[ROWS // 2 :], LANES // 2, axis=1))

    def gram_and_send(peer):
        gram[peer] = gram_of(peer)
        gram_copy(peer, me).start()

    each_peer(lambda peer: when_owner(peer, lambda: gram_and_send(peer)))

    def solve_own():
        grams[me] = gram_of(me)
        each_peer(lambda peer: gram_copy(lax.rem(me, owners), peer).wait_recv())
        summed = jnp.sum(grams[...], axis=0)
        summed = jnp.concatenate([summed, pltpu.roll(summed, LANES // 2, axis=1)], axis=0)
        systems = [summed] + [
            pltpu.roll(summed, LANES - i * ROWS, axis=1) for i in range(1, per_owner)
        ]
        values = solve_systems(jnp.stack(systems, axis=0))
        merged = jnp.zeros((1, LANES), jnp.float32)
        for i in range(per_owner):
            as_row = jnp.sum(jnp.where(diagonal, values[i], 0.0), axis=0, keepdims=True)
            merged = merged + (pltpu.roll(as_row, i * ROWS, axis=1) if i else as_row)
        solved[...] = merged
        arrived_solved[me] = merged
        each_peer(lambda peer: solved_copy(peer, me).start())

    when_owner(me, solve_own)
    each_peer(lambda peer: when_owner(peer, lambda: solved_copy(peer, peer).wait_recv()))
    for v in range(VIS_DEV):
        i = v % per_owner
        as_row = arrived_solved[v // per_owner]
        as_row = pltpu.roll(as_row, LANES - i * ROWS, axis=1) if i else as_row
        coefficient_ref[v : v + 1, :] = as_row
        spread[v] = jnp.broadcast_to(
            jnp.sum(jnp.where(diagonal, as_row, 0.0), axis=1, keepdims=True), (ROWS, LANES)
        )

    def model_of(peer):
        for n in range(capacity):
            s = peer * capacity + n
            values = spread[routes[peer, 0, n]]
            at = peer * model_peer + n // group * model_chunk + n % group * 2
            for i in range(2):
                stage[pl.ds(at + i, 1), :] = jnp.sum(
                    picked[s, i * ROWS : (i + 1) * ROWS, :] * values, axis=0, keepdims=True
                )
        return stage[rows_of(peer, model_peer), :].astype(jnp.bfloat16)

    def model_and_send(peer):
        model_packed[rows_of(peer, model_peer), :] = model_of(peer)
        model_copy(peer, me).start()

    each_peer(model_and_send)
    returned[rows_of(me, model_peer), :] = model_of(me)
    template_copy(0, far, my_visit).wait_send()
    template_copy(1, near, my_visit).wait_send()
    template_copy(2, near, far).wait_send()

    def finish(peer):
        details_copy(peer, me).wait_send()
        tile_copy(peer, me).wait_send()
        when_owner(peer, lambda: gram_copy(peer, me).wait_send())
        when_owner(me, lambda: solved_copy(peer, me).wait_send())
        model_copy(peer, me).wait_send()
        model_copy(peer, peer).wait_recv()

    each_peer(finish)
    stage[: returned.shape[0], :] = returned[...].astype(jnp.float32)

    def give_back(q, carry):
        for t in range(2 * GROUP):
            tile = q * 2 * GROUP + t
            model_ref[tile] = stage[pl.ds(local[0, 7, tile], 2), :]
        return carry

    lax.fori_loop(0, model_ref.shape[0] // (2 * GROUP), give_back, 0)


def per_device(science, inverse_sigma, template, destination, offsets, visit_local):
    patches = lax.axis_size("patch")
    visit_parts = lax.axis_size("visit")
    tile_count, row_count, column_count = science.shape
    capacity = max(2, 2 * tile_count // patches)
    slot_count = patches * capacity
    patch_rows, patch_columns = template.shape[1] * visit_parts, template.shape[2]
    start_rows = -(-(patch_rows - 2 * KR) // 16) * 16
    image_rows = start_rows + 8
    row_band, column_band = band_tables(start_rows, patch_rows)
    group = min(GROUP, capacity)
    tile_total = slot_count // group * chunk_rows(group, 4)
    model_total = slot_count // group * chunk_rows(group, 2)

    owners = min(patches, VIS_DEV)
    vmem = pl.BlockSpec(memory_space=pltpu.VMEM)
    dma = pltpu.SemaphoreType.DMA
    wide, half = jnp.float32, jnp.bfloat16
    own_model, coefficients = pl.pallas_call(
        functools.partial(image_kernel, patches, visit_parts, capacity),
        out_shape=(
            jax.ShapeDtypeStruct(science.shape, wide),
            jax.ShapeDtypeStruct((VIS_DEV, LANES), wide),
        ),
        in_specs=[vmem] * 6 + [pl.BlockSpec(memory_space=pl.ANY)] * 2,
        out_specs=(vmem, vmem),
        scratch_shapes=[
            pltpu.VMEM((patch_rows, patch_columns), half),
            pltpu.VMEM((tile_total, LANES), half),
            pltpu.VMEM((patches, 2, LANES), jnp.int32),
            pltpu.SMEM((patches, 2, LANES), jnp.int32),
            pltpu.VMEM((patches, 2, LANES), jnp.int32),
            pltpu.VMEM((slot_count // LANES, 8, LANES), jnp.int32),
            pltpu.SMEM((slot_count // LANES, 8, LANES), jnp.int32),
            pltpu.VMEM(row_band.shape, half),
            pltpu.VMEM(column_band.shape, half),
            pltpu.VMEM((tile_total, LANES), wide),
            pltpu.VMEM((tile_total, LANES), half),
            pltpu.VMEM((NF, start_rows, patch_columns + LANES), half),
            pltpu.VMEM((patch_columns // LANES, image_rows * ROWS, LANES), wide),
            pltpu.VMEM((slot_count, row_count * ROWS, LANES), wide),
            pltpu.VMEM((slot_count + 1, ROWS, LANES), wide),
            pltpu.VMEM((owners, ROWS // 2, LANES), wide),
            pltpu.VMEM((patches, ROWS // 2, LANES), wide),
            pltpu.VMEM((1, LANES), wide),
            pltpu.VMEM((owners, 1, LANES), wide),
            pltpu.VMEM((VIS_DEV, ROWS, LANES), wide),
            pltpu.VMEM((model_total, LANES), half),
            pltpu.VMEM((model_total, LANES), half),
            dma((2,)),
            dma((2,)),
            dma((3,)),
            dma((3,)),
            dma((patches,)),
            dma((patches,)),
            dma((patches,)),
            dma((patches,)),
            dma((owners,)),
            dma((patches,)),
            dma((patches,)),
            dma((owners,)),
            dma((patches,)),
            dma((patches,)),
        ],
        compiler_params=pltpu.CompilerParams(
            vmem_limit_bytes=VMEM_BYTES, collective_id=0, has_side_effects=True
        ),
    )(
        destination.reshape(1, tile_count),
        visit_local.reshape(1, tile_count),
        offsets.T,
        template[0],
        science,
        inverse_sigma,
        row_band,
        column_band,
    )
    return (science - own_model, coefficients[:, :NB])


def solution(mesh):
    return jax.shard_map(
        per_device,
        mesh=mesh,
        in_specs=(
            P(("patch", "visit"), None, None),
            P(("patch", "visit"), None, None),
            P("patch", "visit", None),
            P(("patch", "visit")),
            P(("patch", "visit"), None),
            P(("patch", "visit")),
        ),
        out_specs=(P(("patch", "visit"), None, None), P("visit", None)),
        check_vma=False,
    )
```
